512 devices in a mesh: seq: 64 (over z, y_lo, core), chan: 8 (over y_hi, x).
Axes of the slice: x: 4, y: 4 (y_hi: 2, y_lo: 2; y = y_hi * 2 + y_lo), z: 16, core: 2. Of those that a mesh axis runs over, the one named last changes fastest.
Arguments:
- query: bfloat16 [8192, 3072], P('seq', 'chan'), may hold values from -6 to 6
- key_in: bfloat16 [8192, 3072], P('seq', 'chan'), may hold values from -6 to 6
- value: bfloat16 [8192, 3072], P('seq', 'chan'), may hold values from -6 to 6
- cotangent: bfloat16 [8192, 3072], P('seq', 'chan'), may hold values from -6 to 6
- filter_raw: bfloat16 [8192, 128], P('seq'), may hold values from -6 to 6
Outputs:
- grad_query: bfloat16 [8192, 3072], P('seq', 'chan')
- grad_key: bfloat16 [8192, 3072], P('seq', 'chan')
- grad_value: bfloat16 [8192, 3072], P('seq', 'chan')
- grad_filter: float32 [8192, 128], P(('seq', 'chan'))
The draws below stay inside these ranges and needn't reach their ends.
All inputs are finite; a program needn't handle non-finite values.
Results may differ from the reference program's by a relative error of at most 0.012.
Values may be sent and summed in bfloat16 or wider, within the bound.
No kernel may reach another device: no remote copies, remote signals or barrier semaphores. Data moves between devices by JAX's collectives and lax.ppermute only.
A program may use at most 64 MiB of HBM per device.

```python
import math
import jax
import jax.numpy as jnp
from jax import lax

D = 3072
FILT = 128
LENGTH = 8192


def steps_of(key, extent, split, smallest, largest):
    gain = 1.0
    for position, shards_of in split:
        draws = jax.random.uniform(jax.random.fold_in(jax.random.fold_in(key, 6), position), (shards_of,), jnp.float32, smallest / len(split), largest / len(split))
        gain = gain * jnp.repeat(jnp.exp(draws), extent[position] // shards_of).reshape((-1,) + (1,) * (len(extent) - 1 - position))
    return gain


def bell_draw(stream_key, extent, width, most, shards=(), held_as=jnp.bfloat16):
    values = jax.random.normal(stream_key, extent, jnp.float32) * width
    if len(shards) > 0:
        values = steps_of(stream_key, extent, shards, -0.22, 0.18) * values
    return jnp.clip(values, min=-most, max=most).astype(held_as)


def setup_inputs(seed: int = 0) -> dict:
    key_of = jax.random.split(jax.random.key(seed), 6)
    query = bell_draw(key_of[0], (LENGTH, D), 1.0, 6.0, ((0, 64), (1, 8)))
    key_in = bell_draw(key_of[1], (LENGTH, D), 1.0, 6.0, ((0, 64), (1, 8)))
    value = bell_draw(key_of[2], (LENGTH, D), 1.0, 6.0, ((0, 64), (1, 8)))
    cotangent = bell_draw(key_of[3], (LENGTH, D), 1.0, 6.0, ((0, 64), (1, 8)))
    filter_raw = bell_draw(key_of[4], (LENGTH, FILT), 1.0, 6.0, ((0, 64),))
    return dict(query=query, key_in=key_in, value=value, cotangent=cotangent, filter_raw=filter_raw)


def reference(query, key_in, value, cotangent, filter_raw):
    length = query.shape[0]
    padded = 2 * length
    blocks = query.shape[1] // FILT
    filt = filter_raw.astype(jnp.float32) * (1.0 / math.sqrt(length))
    filt_spec = jnp.fft.rfft(filt, n=padded, axis=0)

    def regroup(array):
        return jnp.transpose(array.reshape(length, blocks, FILT), (1, 0, 2))

    def step(carry, pieces):
        q_blk, k_blk, v_blk, g_blk = pieces
        mixed = (k_blk.astype(jnp.float32) * v_blk.astype(jnp.float32)).astype(jnp.bfloat16)
        gated = (g_blk.astype(jnp.float32) * q_blk.astype(jnp.float32)).astype(jnp.bfloat16)
        mixed_spec = jnp.fft.rfft(mixed.astype(jnp.float32), n=padded, axis=0)
        gated_spec = jnp.fft.rfft(gated.astype(jnp.float32), n=padded, axis=0)
        conv = jnp.fft.irfft(mixed_spec * filt_spec, n=padded, axis=0)[:length].astype(jnp.bfloat16)
        back_conv = jnp.fft.irfft(gated_spec * jnp.conj(filt_spec), n=padded, axis=0)[:length].astype(jnp.bfloat16)
        grad_q = (g_blk.astype(jnp.float32) * conv.astype(jnp.float32)).astype(jnp.bfloat16)
        grad_k = (back_conv.astype(jnp.float32) * v_blk.astype(jnp.float32)).astype(jnp.bfloat16)
        grad_v = (back_conv.astype(jnp.float32) * k_blk.astype(jnp.float32)).astype(jnp.bfloat16)
        return (carry + gated_spec * jnp.conj(mixed_spec), (grad_q, grad_k, grad_v))
    start = jnp.zeros(filt_spec.shape, filt_spec.dtype)
    cross, grads = lax.scan(step, start, (regroup(query), regroup(key_in), regroup(value), regroup(cotangent)))

    def restore(array):
        return jnp.transpose(array, (1, 0, 2)).reshape(length, blocks * FILT)
    grad_filter = jnp.fft.irfft(cross, n=padded, axis=0)[:length] * (1.0 / math.sqrt(length))
    return (restore(grads[0]), restore(grads[1]), restore(grads[2]), grad_filter.astype(jnp.float32))
```

```python
import math

import numpy as np
import jax
import jax.numpy as jnp
from jax import lax
from jax.experimental import pallas as pl
from jax.experimental.pallas import tpu as pltpu
from jax.sharding import PartitionSpec as P

F32 = jnp.float32
BF16 = jnp.bfloat16
VMEM_LIMIT = 48 * 1024 * 1024


def split_table(table):
    high = table.astype(BF16)
    low = (table - high.astype(np.float64)).astype(BF16)
    return high, low


def make_tables(blocks, width):
    length = blocks * width
    j = np.arange(blocks)
    k1 = np.arange(blocks) + 0.25
    r = np.arange(width)
    k2 = np.arange(width)
    angle_a = 2.0 * np.pi * np.outer(k1, j) / blocks
    outer_t = np.concatenate([np.cos(angle_a), -np.sin(angle_a)], 0)
    angle_t = 2.0 * np.pi * np.outer(k1, r) / length
    twist = np.concatenate([np.cos(angle_t), -np.sin(angle_t)], 1).astype(np.float32)
    angle_b = 2.0 * np.pi * np.outer(r, k2) / width
    cos_b, sin_b = np.cos(angle_b), np.sin(angle_b)
    inner_t = np.block([[cos_b, -sin_b], [sin_b, cos_b]])
    a_hi, a_lo = split_table(outer_t)
    b_hi, b_lo = split_table(inner_t)
    fwd_a = np.concatenate([a_hi, a_lo], 1)
    fwd_b = np.concatenate([b_hi, b_hi, b_lo], 0)
    inv_b = np.concatenate([b_hi.T, b_hi.T, b_lo.T], 0)
    inv_a = np.concatenate([a_hi.T, a_hi.T, a_lo.T], 1)
    return fwd_a, twist, fwd_b, inv_b, inv_a


def split(value):
    high = value.astype(BF16)
    low = (value - high.astype(F32)).astype(BF16)
    return high, low


def mul(left, right):
    return jnp.dot(left, right, preferred_element_type=F32)


def to_spectra(cols, fwd_a, twist, fwd_b):
    blocks, width = cols[0].shape
    data = jnp.concatenate(cols, 1)
    part = mul(fwd_a, jnp.concatenate([data, data], 0))
    t_re, t_im = twist[:, :width], twist[:, width:]
    rows = []
    for s in range(len(cols)):
        a_re = part[:blocks, s * width : (s + 1) * width]
        a_im = part[blocks:, s * width : (s + 1) * width]
        rows.append(jnp.concatenate([a_re * t_re - a_im * t_im, a_re * t_im + a_im * t_re], 1))
    high, low = split(jnp.concatenate(rows, 0))
    return mul(jnp.concatenate([high, low, high], 1), fwd_b)


def from_spectra(spec, twist, inv_b, inv_a, scale):
    blocks = twist.shape[0]
    width = twist.shape[1] // 2
    count = spec.shape[0] // blocks
    high, low = split(spec)
    part = mul(jnp.concatenate([high, low, high], 1), inv_b)
    t_re, t_im = twist[:, :width], twist[:, width:]
    cols = []
    for s in range(count):
        d_re = part[s * blocks : (s + 1) * blocks, :width]
        d_im = part[s * blocks : (s + 1) * blocks, width:]
        cols.append(jnp.concatenate([d_re * t_re + d_im * t_im, d_im * t_re - d_re * t_im], 0))
    high, low = split(jnp.concatenate(cols, 1))
    return mul(inv_a, jnp.concatenate([high, low, high], 0)) * scale


def gate_kernel(repeat, left_ref, right_ref, *refs):
    out_ref, hold = refs[-2], refs[-1]
    width = left_ref.shape[0]
    per = out_ref.shape[0] // hold.shape[0] * 8
    blocks = out_ref.shape[0] // per
    fils = width // blocks
    prod = left_ref[...].astype(F32) * right_ref[...].astype(F32)
    prod = prod.astype(BF16).astype(F32)
    parts = [prod[:, c * width : (c + 1) * width] for c in range(repeat)]
    if len(refs) == 3:
        parts.append(refs[0][...].astype(F32))
    else:
        parts.append(jnp.zeros((width, width), F32))
    for c, part in enumerate(parts):
        flipped = part.T
        for f in range(fils):
            hold[pl.ds(c * fils + f, blocks, stride=per), :] = flipped[f * blocks : (f + 1) * blocks]
    out_ref[...] = hold[...].astype(BF16)


def gate(left, right, *extra):
    width, channels = left.shape
    rows = 64 * 8
    return pl.pallas_call(
        lambda *refs: gate_kernel(channels // width, *refs),
        out_shape=jax.ShapeDtypeStruct((rows, width), BF16),
        scratch_shapes=[pltpu.VMEM((rows, width), F32)],
        compiler_params=pltpu.CompilerParams(vmem_limit_bytes=VMEM_LIMIT),
        name="gate",
    )(left, right, *extra)


def take_columns(ref, hold, per, blocks):
    hold[...] = ref[...].astype(F32)
    return [hold[pl.ds(s, blocks, stride=per), :].astype(BF16) for s in range(per)]


def times(a, b):
    w = a.shape[1] // 2
    a_re, a_im, b_re, b_im = a[:, :w], a[:, w:], b[:, :w], b[:, w:]
    return jnp.concatenate([a_re * b_re - a_im * b_im, a_re * b_im + a_im * b_re], 1)


def times_conj(a, b):
    w = a.shape[1] // 2
    a_re, a_im, b_re, b_im = a[:, :w], a[:, w:], b[:, :w], b[:, w:]
    return jnp.concatenate([a_re * b_re + a_im * b_im, a_im * b_re - a_re * b_im], 1)


def put_rows(out_ref, hold, result, per, count, blocks, width):
    for s in range(count):
        hold[pl.ds(s, blocks, stride=per), :] = result[:, s * width : (s + 1) * width]
    for s in range(count, per):
        hold[pl.ds(s, blocks, stride=per), :] = jnp.zeros((blocks, width), F32)
    out_ref[...] = hold[...].astype(BF16)


def conv_kernel(repeat, fils, scale, x_ref, fa, tw, fb, ib, ia, out_ref, spec_ref, hold):
    blocks = tw.shape[0]
    width = tw.shape[1] // 2
    per = (repeat + 1) * fils
    count = repeat * fils
    cols = take_columns(x_ref, hold, per, blocks)
    spec = to_spectra(cols, fa[...], tw[...], fb[...])
    spec_ref[...] = spec
    taps = spec[count * blocks :]
    prods = [times(spec[s * fils * blocks : (s + 1) * fils * blocks], taps) for s in range(repeat)]
    result = from_spectra(jnp.concatenate(prods, 0), tw[...], ib[...], ia[...], scale)
    put_rows(out_ref, hold, result, per, count, blocks, width)


def back_kernel(repeat, fils, scale, x_ref, spec_ref, fa, tw, fb, ib, ia, out_ref, hold):
    blocks = tw.shape[0]
    width = tw.shape[1] // 2
    per = (repeat + 1) * fils
    count = repeat * fils
    cols = take_columns(x_ref, hold, per, blocks)[:count]
    spec = to_spectra(cols, fa[...], tw[...], fb[...])
    step = fils * blocks
    taps = spec_ref[count * blocks :]
    prods = []
    cross = None
    for s in range(repeat):
        gated = spec[s * step : (s + 1) * step]
        prods.append(times_conj(gated, taps))
        term = times_conj(gated, spec_ref[s * step : (s + 1) * step])
        cross = term if cross is None else cross + term
    prods.append(cross)
    result = from_spectra(jnp.concatenate(prods, 0), tw[...], ib[...], ia[...], scale)
    put_rows(out_ref, hold, result, per, per, blocks, width)


def back_rows(hold, per, blocks, width, c):
    fils = width // blocks
    rows = [hold[pl.ds(c * fils + f, blocks, stride=per), :] for f in range(fils)]
    return jnp.concatenate(rows, 0).T


def query_kernel(repeat, conv_ref, cot_ref, out_ref, hold):
    width = cot_ref.shape[0]
    per = conv_ref.shape[0] // 64
    hold[...] = conv_ref[...].astype(F32)
    for c in range(repeat):
        at = slice(c * width, (c + 1) * width)
        conv = back_rows(hold, per, 64, width, c)
        out_ref[:, at] = (cot_ref[:, at].astype(F32) * conv).astype(BF16)


def input_kernel(repeat, back_ref, value_ref, key_ref, grad_key, grad_value, taps_ref, hold):
    width = value_ref.shape[0]
    per = back_ref.shape[0] // 64
    hold[...] = back_ref[...].astype(F32)
    taps_ref[...] = back_rows(hold, per, 64, width, repeat).astype(BF16)
    for c in range(repeat):
        at = slice(c * width, (c + 1) * width)
        back = back_rows(hold, per, 64, width, c)
        grad_key[:, at] = (back * value_ref[:, at].astype(F32)).astype(BF16)
        grad_value[:, at] = (back * key_ref[:, at].astype(F32)).astype(BF16)


def sum_kernel(part_ref, out_ref):
    rows = out_ref.shape[0]
    total = part_ref[:rows].astype(F32)
    for c in range(1, part_ref.shape[0] // rows):
        total = total + part_ref[c * rows : (c + 1) * rows].astype(F32)
    out_ref[...] = total


def local(query, key_in, value, cotangent, filter_raw):
    width, channels = query.shape
    blocks = lax.axis_size("seq")
    groups = lax.axis_size("chan")
    length = blocks * width
    filters = filter_raw.shape[1]
    repeat = channels // filters
    fils = filters // blocks
    per = (repeat + 1) * fils
    scale = 1.0 / (length * math.sqrt(length))
    fwd_a, twist, fwd_b, inv_b, inv_a = (jnp.asarray(t) for t in make_tables(blocks, width))
    params = pltpu.CompilerParams(vmem_limit_bytes=VMEM_LIMIT)
    packed = jax.ShapeDtypeStruct((blocks * per, width), BF16)
    hold = pltpu.VMEM((blocks * per, width), F32)

    def swap(array, axis):
        return lax.all_to_all(array, axis, split_axis=0, concat_axis=0, tiled=True)

    mixed = swap(gate(key_in, value, filter_raw), "seq")
    gated = swap(gate(cotangent, query), "seq")
    conv, spec = pl.pallas_call(
        lambda *refs: conv_kernel(repeat, fils, scale, *refs),
        out_shape=(packed, jax.ShapeDtypeStruct((per * blocks, 2 * width), F32)),
        scratch_shapes=[hold],
        compiler_params=params,
        name="conv",
    )(mixed, fwd_a, twist, fwd_b, inv_b, inv_a)
    conv = swap(conv, "seq")
    back = pl.pallas_call(
        lambda *refs: back_kernel(repeat, fils, scale, *refs),
        out_shape=packed,
        scratch_shapes=[hold],
        compiler_params=params,
        name="back",
    )(gated, spec, fwd_a, twist, fwd_b, inv_b, inv_a)
    back = swap(back, "seq")
    like = jax.ShapeDtypeStruct((width, channels), BF16)
    grad_query = pl.pallas_call(
        lambda *refs: query_kernel(repeat, *refs),
        out_shape=like,
        scratch_shapes=[hold],
        compiler_params=params,
        name="grad_query",
    )(conv, cotangent)
    grad_key, grad_value, taps = pl.pallas_call(
        lambda *refs: input_kernel(repeat, *refs),
        out_shape=(like, like, jax.ShapeDtypeStruct((width, filters), BF16)),
        scratch_shapes=[hold],
        compiler_params=params,
        name="grad_inputs",
    )(back, value, key_in)
    taps = swap(taps, "chan")
    grad_filter = pl.pallas_call(
        sum_kernel,
        out_shape=jax.ShapeDtypeStruct((width // groups, filters), F32),
        compiler_params=params,
        name="grad_filter",
    )(taps)
    return (grad_query, grad_key, grad_value, grad_filter)


def solution(mesh):
    placed = (
        P("seq", "chan"),
        P("seq", "chan"),
        P("seq", "chan"),
        P("seq", "chan"),
        P("seq", None),
    )
    return jax.shard_map(
        local,
        mesh=mesh,
        in_specs=placed,
        out_specs=(P("seq", "chan"), P("seq", "chan"), P("seq", "chan"), P(("seq", "chan"), None)),
        check_vma=False,
    )
```

```python
import functools
import math

import numpy as np
import jax
import jax.numpy as jnp
from jax import lax
from jax.experimental import pallas as pl
from jax.experimental.pallas import tpu as pltpu
from jax.sharding import PartitionSpec as P

F32 = jnp.float32
BF16 = jnp.bfloat16
VMEM_LIMIT = 48 * 1024 * 1024


def split_table(table):
    high = table.astype(BF16)
    low = (table - high.astype(np.float64)).astype(BF16)
    return high, low


def make_tables(blocks, width):
    length = blocks * width
    j = np.arange(blocks)
    k1 = np.arange(blocks) + 0.25
    r = np.arange(width)
    k2 = np.arange(width)
    angle_a = 2.0 * np.pi * np.outer(k1, j) / blocks
    outer_t = np.concatenate([np.cos(angle_a), -np.sin(angle_a)], 0)
    angle_t = 2.0 * np.pi * np.outer(k1, r) / length
    twist = np.concatenate([np.cos(angle_t), -np.sin(angle_t)], 1).astype(np.float32)
    angle_b = 2.0 * np.pi * np.outer(r, k2) / width
    cos_b, sin_b = np.cos(angle_b), np.sin(angle_b)
    inner_t = np.block([[cos_b, -sin_b], [sin_b, cos_b]])
    a_hi, a_lo = split_table(outer_t)
    b_hi, b_lo = split_table(inner_t)
    fwd_a = np.concatenate([a_hi, a_lo], 1)
    fwd_b = np.concatenate([b_hi, b_hi, b_lo], 0)
    inv_b = np.concatenate([b_hi.T, b_hi.T, b_lo.T], 0)
    inv_a = np.concatenate([a_hi.T, a_hi.T, a_lo.T], 1)
    return fwd_a, twist, fwd_b, inv_b, inv_a


def split(value):
    high = value.astype(BF16)
    low = (value - high.astype(F32)).astype(BF16)
    return high, low


def mul(left, right):
    return jnp.dot(left, right, preferred_element_type=F32)


def to_spectra(cols, fwd_a, twist, fwd_b):
    blocks, width = cols[0].shape
    data = jnp.concatenate(cols, 1)
    part = mul(fwd_a, jnp.concatenate([data, data], 0))
    t_re, t_im = twist[:, :width], twist[:, width:]
    rows = []
    for s in range(len(cols)):
        a_re = part[:blocks, s * width : (s + 1) * width]
        a_im = part[blocks:, s * width : (s + 1) * width]
        rows.append(jnp.concatenate([a_re * t_re - a_im * t_im, a_re * t_im + a_im * t_re], 1))
    high, low = split(jnp.concatenate(rows, 0))
    return mul(jnp.concatenate([high, low, high], 1), fwd_b)


def from_spectra(spec, twist, inv_b, inv_a, scale):
    blocks = twist.shape[0]
    width = twist.shape[1] // 2
    count = spec.shape[0] // blocks
    high, low = split(spec)
    part = mul(jnp.concatenate([high, low, high], 1), inv_b)
    t_re, t_im = twist[:, :width], twist[:, width:]
    cols = []
    for s in range(count):
        d_re = part[s * blocks : (s + 1) * blocks, :width]
        d_im = part[s * blocks : (s + 1) * blocks, width:]
        cols.append(jnp.concatenate([d_re * t_re + d_im * t_im, d_im * t_re - d_re * t_im], 0))
    high, low = split(jnp.concatenate(cols, 1))
    return mul(inv_a, jnp.concatenate([high, low, high], 0)) * scale


def gate_kernel(repeat, blocks, query, key_in, value, cotangent, taps, out_ref, *scratch):
    hold, sems = scratch[-2], scratch[-1]
    width = taps.shape[0]
    fils = width // blocks
    per = (2 * repeat + 1) * fils
    copies = []
    for i, source in enumerate((key_in, value, taps, cotangent, query)):
        copies.append(pltpu.make_async_copy(source, scratch[i], sems.at[i]))
        copies[-1].start()
    k_in, v_in, t_in, g_in, q_in = scratch[:5]

    def put(first, part):
        flipped = part.T
        for f in range(fils):
            hold[pl.ds(first + f, blocks, stride=per), :] = flipped[f * blocks : (f + 1) * blocks]

    def put_product(first, left, right):
        for c in range(repeat):
            at = slice(c * width, (c + 1) * width)
            prod = left[:, at].astype(F32) * right[:, at].astype(F32)
            put(first + c * fils, prod.astype(BF16).astype(F32))

    copies[0].wait()
    copies[1].wait()
    put_product(0, k_in, v_in)
    copies[2].wait()
    put(2 * repeat * fils, t_in[...].astype(F32))
    copies[3].wait()
    copies[4].wait()
    put_product(repeat * fils, g_in, q_in)
    out_ref[...] = hold[...].astype(BF16)


def take_columns(ref, hold, per, blocks):
    hold[...] = ref[...].astype(F32)
    return [hold[pl.ds(s, blocks, stride=per), :].astype(BF16) for s in range(per)]


def times(a, b):
    w = a.shape[1] // 2
    a_re, a_im, b_re, b_im = a[:, :w], a[:, w:], b[:, :w], b[:, w:]
    return jnp.concatenate([a_re * b_re - a_im * b_im, a_re * b_im + a_im * b_re], 1)


def times_conj(a, b):
    w = a.shape[1] // 2
    a_re, a_im, b_re, b_im = a[:, :w], a[:, w:], b[:, :w], b[:, w:]
    return jnp.concatenate([a_re * b_re + a_im * b_im, a_im * b_re - a_re * b_im], 1)


def core_kernel(repeat, scale, x_ref, fa, tw, fb, ib, ia, out_ref, hold):
    blocks = tw.shape[0]
    width = tw.shape[1] // 2
    per = x_ref.shape[0] // blocks
    fils = per // (2 * repeat + 1)
    step = fils * blocks
    spec = to_spectra(take_columns(x_ref, hold, per, blocks), fa[...], tw[...], fb[...])
    parts = [spec[s * step : (s + 1) * step] for s in range(2 * repeat + 1)]
    mixed, gated, taps = parts[:repeat], parts[repeat : 2 * repeat], parts[-1]
    cross = times_conj(gated[0], mixed[0])
    for s in range(1, repeat):
        cross = cross + times_conj(gated[s], mixed[s])
    prods = [times(m, taps) for m in mixed] + [times_conj(g, taps) for g in gated] + [cross]
    result = from_spectra(jnp.concatenate(prods, 0), tw[...], ib[...], ia[...], scale)
    for s in range(per):
        hold[pl.ds(s, blocks, stride=per), :] = result[:, s * width : (s + 1) * width]
    out_ref[...] = hold[...].astype(BF16)


def back_rows(rows, first, blocks, width):
    per = rows.shape[0] // blocks
    parts = [rows[pl.ds(first + f, blocks, stride=per), :] for f in range(width // blocks)]
    return jnp.concatenate(parts, 0).T


def taps_kernel(repeat, blocks, rows_ref, taps_ref, hold):
    width = taps_ref.shape[0]
    hold[...] = rows_ref[...].astype(F32)
    taps_ref[...] = back_rows(hold, 2 * repeat * (width // blocks), blocks, width).astype(BF16)


def grads_kernel(repeat, blocks, rows_ref, cot, value, key_in, grad_query, grad_key, grad_value, hold):
    width = cot.shape[0]
    fils = width // blocks
    hold[...] = rows_ref[...].astype(F32)
    for c in range(repeat):
        at = slice(c * width, (c + 1) * width)
        conv = back_rows(hold, c * fils, blocks, width)
        grad_query[:, at] = (cot[:, at].astype(F32) * conv).astype(BF16)
        back = back_rows(hold, (repeat + c) * fils, blocks, width)
        grad_key[:, at] = (back * value[:, at].astype(F32)).astype(BF16)
        grad_value[:, at] = (back * key_in[:, at].astype(F32)).astype(BF16)


def sum_kernel(part_ref, out_ref):
    rows = out_ref.shape[0]
    total = part_ref[:rows].astype(F32)
    for c in range(1, part_ref.shape[0] // rows):
        total = total + part_ref[c * rows : (c + 1) * rows].astype(F32)
    out_ref[...] = total


def local(query, key_in, value, cotangent, filter_raw):
    width, channels = query.shape
    blocks = lax.axis_size("seq")
    groups = lax.axis_size("chan")
    length = blocks * width
    filters = filter_raw.shape[1]
    repeat = channels // filters
    fils = filters // blocks
    per = (2 * repeat + 1) * fils
    scale = 1.0 / (length * math.sqrt(length))
    tables = [jnp.asarray(t) for t in make_tables(blocks, width)]
    params = pltpu.CompilerParams(vmem_limit_bytes=VMEM_LIMIT)
    packed = jax.ShapeDtypeStruct((blocks * per, width), BF16)
    hold = pltpu.VMEM((blocks * per, width), F32)

    def swap(array):
        shape = (blocks, per // fils, fils, width)
        moved = lax.all_to_all(array.reshape(shape), "seq", split_axis=0, concat_axis=0, tiled=True)
        return moved.reshape(array.shape)

    wide = pltpu.VMEM((width, channels), BF16)
    rows = pl.pallas_call(
        functools.partial(gate_kernel, repeat, blocks),
        out_shape=packed,
        in_specs=[pl.BlockSpec(memory_space=pl.ANY)] * 5,
        scratch_shapes=[wide, wide, pltpu.VMEM((width, filters), BF16), wide, wide, hold, pltpu.SemaphoreType.DMA((5,))],
        compiler_params=params,
        name="gate",
    )(query, key_in, value, cotangent, filter_raw)
    rows = pl.pallas_call(
        functools.partial(core_kernel, repeat, scale),
        out_shape=packed,
        scratch_shapes=[hold],
        compiler_params=params,
        name="core",
    )(swap(rows), *tables)
    rows = swap(rows)
    taps = pl.pallas_call(
        functools.partial(taps_kernel, repeat, blocks),
        out_shape=jax.ShapeDtypeStruct((width, filters), BF16),
        scratch_shapes=[hold],
        compiler_params=params,
        name="taps",
    )(rows)
    taps = lax.all_to_all(taps, "chan", split_axis=0, concat_axis=0, tiled=True)
    like = jax.ShapeDtypeStruct((width, channels), BF16)
    grads = pl.pallas_call(
        functools.partial(grads_kernel, repeat, blocks),
        out_shape=(like, like, like),
        scratch_shapes=[hold],
        compiler_params=params,
        name="grads",
    )(rows, cotangent, value, key_in)
    grad_filter = pl.pallas_call(
        sum_kernel,
        out_shape=jax.ShapeDtypeStruct((width // groups, filters), F32),
        compiler_params=params,
        name="grad_filter",
    )(taps)
    return (*grads, grad_filter)


def solution(mesh):
    placed = (
        P("seq", "chan"),
        P("seq", "chan"),
        P("seq", "chan"),
        P("seq", "chan"),
        P("seq", None),
    )
    return jax.shard_map(
        local,
        mesh=mesh,
        in_specs=placed,
        out_specs=(P("seq", "chan"), P("seq", "chan"), P("seq", "chan"), P(("seq", "chan"), None)),
        check_vma=False,
    )
```

```python
import functools
import math

import numpy as np
import jax
import jax.numpy as jnp
from jax import lax
from jax.experimental import pallas as pl
from jax.experimental.pallas import tpu as pltpu
from jax.sharding import PartitionSpec as P

F32 = jnp.float32
BF16 = jnp.bfloat16
VMEM_LIMIT = 48 * 1024 * 1024


def split_table(table):
    high = table.astype(BF16)
    low = (table - high.astype(np.float64)).astype(BF16)
    return high, low


def make_tables(blocks, width, order):
    length = blocks * width
    j = np.array(order)
    k1 = np.arange(blocks) + 0.25
    r = np.arange(width)
    k2 = np.arange(width)
    angle_a = 2.0 * np.pi * np.outer(k1, j) / blocks
    outer_t = np.concatenate([np.cos(angle_a), -np.sin(angle_a)], 0)
    angle_t = 2.0 * np.pi * np.outer(k1, r) / length
    twist = np.concatenate([np.cos(angle_t), -np.sin(angle_t)], 1).astype(np.float32)
    angle_b = 2.0 * np.pi * np.outer(r, k2) / width
    cos_b, sin_b = np.cos(angle_b), np.sin(angle_b)
    inner_t = np.block([[cos_b, -sin_b], [sin_b, cos_b]])
    a_hi, a_lo = split_table(outer_t)
    b_hi, b_lo = split_table(inner_t)
    fwd_a = np.concatenate([a_hi, a_lo], 1)
    fwd_b = np.concatenate([b_hi, b_hi, b_lo], 0)
    inv_b = np.concatenate([b_hi.T, b_hi.T, b_lo.T], 0)
    inv_a = np.concatenate([a_hi.T, a_hi.T, a_lo.T], 1)
    return fwd_a, twist, fwd_b, inv_b, inv_a


def split(value):
    high = value.astype(BF16)
    low = (value - high.astype(F32)).astype(BF16)
    return high, low


def mul(left, right):
    return jnp.dot(left, right, preferred_element_type=F32)


def to_spectra(cols, fwd_a, twist, fwd_b):
    blocks, width = cols[0].shape
    data = jnp.concatenate(cols, 1)
    part = mul(fwd_a, jnp.concatenate([data, data], 0))
    t_re, t_im = twist[:, :width], twist[:, width:]
    rows = []
    for s in range(len(cols)):
        a_re = part[:blocks, s * width : (s + 1) * width]
        a_im = part[blocks:, s * width : (s + 1) * width]
        rows.append(jnp.concatenate([a_re * t_re - a_im * t_im, a_re * t_im + a_im * t_re], 1))
    high, low = split(jnp.concatenate(rows, 0))
    return mul(jnp.concatenate([high, low, high], 1), fwd_b)


def from_spectra(spec, twist, inv_b, inv_a, scale):
    blocks = twist.shape[0]
    width = twist.shape[1] // 2
    count = spec.shape[0] // blocks
    high, low = split(spec)
    part = mul(jnp.concatenate([high, low, high], 1), inv_b)
    t_re, t_im = twist[:, :width], twist[:, width:]
    cols = []
    for s in range(count):
        d_re = part[s * blocks : (s + 1) * blocks, :width]
        d_im = part[s * blocks : (s + 1) * blocks, width:]
        cols.append(jnp.concatenate([d_re * t_re + d_im * t_im, d_im * t_re - d_re * t_im], 0))
    high, low = split(jnp.concatenate(cols, 1))
    return mul(inv_a, jnp.concatenate([high, low, high], 0)) * scale


def gate_kernel(repeat, blocks, query, key_in, value, cotangent, taps, out_ref, *scratch):
    hold, sems = scratch[-2], scratch[-1]
    width = taps.shape[0]
    fils = width // blocks
    per = (2 * repeat + 1) * fils
    copies = []
    for i, source in enumerate((key_in, value, taps, cotangent, query)):
        copies.append(pltpu.make_async_copy(source, scratch[i], sems.at[i]))
        copies[-1].start()
    k_in, v_in, t_in, g_in, q_in = scratch[:5]

    def put(first, part):
        flipped = part.T
        for f in range(fils):
            hold[pl.ds(first + f, blocks, stride=per), :] = flipped[f * blocks : (f + 1) * blocks]

    def put_product(first, left, right):
        for c in range(repeat):
            at = slice(c * width, (c + 1) * width)
            prod = left[:, at].astype(F32) * right[:, at].astype(F32)
            put(first + c * fils, prod.astype(BF16).astype(F32))

    copies[0].wait()
    copies[1].wait()
    put_product(0, k_in, v_in)
    copies[2].wait()
    put(2 * repeat * fils, t_in[...].astype(F32))
    copies[3].wait()
    copies[4].wait()
    put_product(repeat * fils, g_in, q_in)
    out_ref[...] = hold[...].astype(BF16)


def take_columns(ref, hold, per, blocks):
    hold[...] = ref[...].astype(F32)
    return [hold[pl.ds(s, blocks, stride=per), :].astype(BF16) for s in range(per)]


def times(a, b):
    w = a.shape[1] // 2
    a_re, a_im, b_re, b_im = a[:, :w], a[:, w:], b[:, :w], b[:, w:]
    return jnp.concatenate([a_re * b_re - a_im * b_im, a_re * b_im + a_im * b_re], 1)


def times_conj(a, b):
    w = a.shape[1] // 2
    a_re, a_im, b_re, b_im = a[:, :w], a[:, w:], b[:, :w], b[:, w:]
    return jnp.concatenate([a_re * b_re + a_im * b_im, a_im * b_re - a_re * b_im], 1)


def core_kernel(repeat, scale, x_ref, fa, tw, fb, ib, ia, out_ref, hold):
    blocks = tw.shape[0]
    width = tw.shape[1] // 2
    per = x_ref.shape[0] // blocks
    fils = per // (2 * repeat + 1)
    step = fils * blocks
    spec = to_spectra(take_columns(x_ref, hold, per, blocks), fa[...], tw[...], fb[...])
    parts = [spec[s * step : (s + 1) * step] for s in range(2 * repeat + 1)]
    mixed, gated, taps = parts[:repeat], parts[repeat : 2 * repeat], parts[-1]
    cross = times_conj(gated[0], mixed[0])
    for s in range(1, repeat):
        cross = cross + times_conj(gated[s], mixed[s])
    prods = [times(m, taps) for m in mixed] + [times_conj(g, taps) for g in gated] + [cross]
    result = from_spectra(jnp.concatenate(prods, 0), tw[...], ib[...], ia[...], scale)
    for s in range(per):
        hold[pl.ds(s, blocks, stride=per), :] = result[:, s * width : (s + 1) * width]
    out_ref[...] = hold[...].astype(BF16)


def back_rows(rows, first, blocks, width):
    per = rows.shape[0] // blocks
    parts = [rows[pl.ds(first + f, blocks, stride=per), :] for f in range(width // blocks)]
    return jnp.concatenate(parts, 0).T


def grads_kernel(repeat, blocks, group, rows_ref, cot, value, key_in, grad_query, grad_key, grad_value, taps, hold):
    width = cot.shape[0]
    fils = width // blocks
    hold[...] = rows_ref[...].astype(F32)
    flipped = back_rows(hold, 2 * repeat * fils, blocks, width).astype(BF16)
    lags = width // len(group)
    for c, owner in enumerate(group):
        taps[c * lags : (c + 1) * lags] = flipped[owner * lags : (owner + 1) * lags]
    for c in range(repeat):
        at = slice(c * width, (c + 1) * width)
        conv = back_rows(hold, c * fils, blocks, width)
        grad_query[:, at] = (cot[:, at].astype(F32) * conv).astype(BF16)
        back = back_rows(hold, (repeat + c) * fils, blocks, width)
        grad_key[:, at] = (back * value[:, at].astype(F32)).astype(BF16)
        grad_value[:, at] = (back * key_in[:, at].astype(F32)).astype(BF16)


def sum_kernel(part_ref, out_ref):
    rows = out_ref.shape[0]
    total = part_ref[:rows].astype(F32)
    for c in range(1, part_ref.shape[0] // rows):
        total = total + part_ref[c * rows : (c + 1) * rows].astype(F32)
    out_ref[...] = total


def local(query, key_in, value, cotangent, filter_raw):
    width, channels = query.shape
    blocks = lax.axis_size("seq")
    groups = lax.axis_size("chan")
    length = blocks * width
    filters = filter_raw.shape[1]
    repeat = channels // filters
    fils = filters // blocks
    per = (2 * repeat + 1) * fils
    scale = 1.0 / (length * math.sqrt(length))
    first = blocks // 2 + 2
    group = [(3 * groups // 4 + c) % groups for c in range(groups)]
    order = [(first + i) % blocks for i in range(blocks)]
    tables = [jnp.asarray(t) for t in make_tables(blocks, width, order)]
    params = pltpu.CompilerParams(vmem_limit_bytes=VMEM_LIMIT)
    packed = jax.ShapeDtypeStruct((blocks * per, width), BF16)
    hold = pltpu.VMEM((blocks * per, width), F32)

    def swap(array):
        shape = (blocks, per // fils, fils, width)
        moved = lax.all_to_all(array.reshape(shape), "seq", split_axis=0, concat_axis=0, tiled=True, axis_index_groups=[order])
        return moved.reshape(array.shape)

    wide = pltpu.VMEM((width, channels), BF16)
    rows = pl.pallas_call(
        functools.partial(gate_kernel, repeat, blocks),
        out_shape=packed,
        in_specs=[pl.BlockSpec(memory_space=pl.ANY)] * 5,
        scratch_shapes=[wide, wide, pltpu.VMEM((width, filters), BF16), wide, wide, hold, pltpu.SemaphoreType.DMA((5,))],
        name="gate",
    )(query, key_in, value, cotangent, filter_raw)
    rows = pl.pallas_call(
        functools.partial(core_kernel, repeat, scale),
        out_shape=packed,
        scratch_shapes=[hold],
        compiler_params=params,
        name="core",
    )(swap(rows), *tables)
    rows = swap(rows)
    like = jax.ShapeDtypeStruct((width, channels), BF16)
    *grads, taps = pl.pallas_call(
        functools.partial(grads_kernel, repeat, blocks, group),
        out_shape=(like, like, like, jax.ShapeDtypeStruct((width, filters), BF16)),
        scratch_shapes=[hold],
        compiler_params=params,
        name="grads",
    )(rows, cotangent, value, key_in)
    taps = lax.all_to_all(taps, "chan", split_axis=0, concat_axis=0, tiled=True, axis_index_groups=[group])
    grad_filter = pl.pallas_call(
        sum_kernel,
        out_shape=jax.ShapeDtypeStruct((width // groups, filters), F32),
        compiler_params=params,
        name="grad_filter",
    )(taps)
    return (*grads, grad_filter)


def solution(mesh):
    placed = (
        P("seq", "chan"),
        P("seq", "chan"),
        P("seq", "chan"),
        P("seq", "chan"),
        P("seq", None),
    )
    return jax.shard_map(
        local,
        mesh=mesh,
        in_specs=placed,
        out_specs=(P("seq", "chan"), P("seq", "chan"), P("seq", "chan"), P(("seq", "chan"), None)),
        check_vma=False,
    )
```

```python
import functools
import math

import numpy as np
import jax
import jax.numpy as jnp
from jax import lax
from jax.experimental import pallas as pl
from jax.experimental.pallas import tpu as pltpu
from jax.sharding import PartitionSpec as P

F32 = jnp.float32
BF16 = jnp.bfloat16
VMEM_LIMIT = 48 * 1024 * 1024


def split_table(table):
    high = table.astype(BF16)
    low = (table - high.astype(np.float64)).astype(BF16)
    return high, low


def make_tables(blocks, width, order):
    length = blocks * width
    j = np.array(order)
    k1 = np.arange(blocks) + 0.25
    r = np.arange(width)
    k2 = np.arange(width)
    angle_a = 2.0 * np.pi * np.outer(k1, j) / blocks
    outer_t = np.concatenate([np.cos(angle_a), -np.sin(angle_a)], 0)
    angle_t = 2.0 * np.pi * np.outer(k1, r) / length
    twist = np.concatenate([np.cos(angle_t), -np.sin(angle_t)], 1).astype(np.float32)
    angle_b = 2.0 * np.pi * np.outer(r, k2) / width
    cos_b, sin_b = np.cos(angle_b), np.sin(angle_b)
    inner_t = np.block([[cos_b, -sin_b], [sin_b, cos_b]])
    a_hi, a_lo = split_table(outer_t)
    b_hi, b_lo = split_table(inner_t)
    fwd_a = np.concatenate([a_hi, a_lo], 1)
    fwd_b = np.concatenate([b_hi, b_hi, b_lo], 0)
    return fwd_a, twist, fwd_b, b_hi.T, a_hi.T


def split(value):
    high = value.astype(BF16)
    low = (value - high.astype(F32)).astype(BF16)
    return high, low


def mul(left, right):
    return jnp.dot(left, right, preferred_element_type=F32)


def to_spectra(cols, fwd_a, twist, fwd_b):
    blocks, width = cols[0].shape
    data = jnp.concatenate(cols, 1)
    part = mul(fwd_a, jnp.concatenate([data, data], 0))
    t_re, t_im = twist[:, :width], twist[:, width:]
    rows = []
    for s in range(len(cols)):
        a_re = part[:blocks, s * width : (s + 1) * width]
        a_im = part[blocks:, s * width : (s + 1) * width]
        rows.append(jnp.concatenate([a_re * t_re - a_im * t_im, a_re * t_im + a_im * t_re], 1))
    high, low = split(jnp.concatenate(rows, 0))
    return mul(jnp.concatenate([high, low, high], 1), fwd_b)


def from_spectra(spec, twist, inv_b, inv_a, scale):
    blocks = twist.shape[0]
    width = twist.shape[1] // 2
    count = spec.shape[0] // blocks
    part = mul(spec.astype(BF16), inv_b)
    t_re, t_im = twist[:, :width], twist[:, width:]
    cols = []
    for s in range(count):
        d_re = part[s * blocks : (s + 1) * blocks, :width]
        d_im = part[s * blocks : (s + 1) * blocks, width:]
        cols.append(jnp.concatenate([d_re * t_re + d_im * t_im, d_im * t_re - d_re * t_im], 0))
    return mul(inv_a, jnp.concatenate(cols, 1).astype(BF16)) * scale


def gate_kernel(repeat, blocks, query, key_in, value, cotangent, taps, out_ref, *scratch):
    hold, sems = scratch[-2], scratch[-1]
    width = taps.shape[0]
    fils = width // blocks
    per = (2 * repeat + 1) * fils
    copies = []
    for i, source in enumerate((key_in, value, taps, cotangent, query)):
        copies.append(pltpu.make_async_copy(source, scratch[i], sems.at[i]))
        copies[-1].start()
    k_in, v_in, t_in, g_in, q_in = scratch[:5]

    def put(first, part):
        flipped = part.T
        for f in range(fils):
            hold[pl.ds(first + f, blocks, stride=per), :] = flipped[f * blocks : (f + 1) * blocks]

    def put_product(first, left, right):
        for c in range(repeat):
            at = slice(c * width, (c + 1) * width)
            prod = left[:, at].astype(F32) * right[:, at].astype(F32)
            put(first + c * fils, prod.astype(BF16).astype(F32))

    copies[0].wait()
    copies[1].wait()
    put_product(0, k_in, v_in)
    copies[2].wait()
    put(2 * repeat * fils, t_in[...].astype(F32))
    copies[3].wait()
    copies[4].wait()
    put_product(repeat * fils, g_in, q_in)
    out_ref[...] = hold[...].astype(BF16)


def take_columns(ref, hold, per, blocks):
    hold[...] = ref[...].astype(F32)
    return [hold[pl.ds(s, blocks, stride=per), :].astype(BF16) for s in range(per)]


def times(a, b):
    w = a.shape[1] // 2
    a_re, a_im, b_re, b_im = a[:, :w], a[:, w:], b[:, :w], b[:, w:]
    return jnp.concatenate([a_re * b_re - a_im * b_im, a_re * b_im + a_im * b_re], 1)


def times_conj(a, b):
    w = a.shape[1] // 2
    a_re, a_im, b_re, b_im = a[:, :w], a[:, w:], b[:, :w], b[:, w:]
    return jnp.concatenate([a_re * b_re + a_im * b_im, a_im * b_re - a_re * b_im], 1)


def core_kernel(repeat, scale, x_ref, fa, tw, fb, ib, ia, out_ref, hold):
    blocks = tw.shape[0]
    width = tw.shape[1] // 2
    per = x_ref.shape[0] // blocks
    fils = per // (2 * repeat + 1)
    step = fils * blocks
    spec = to_spectra(take_columns(x_ref, hold, per, blocks), fa[...], tw[...], fb[...])
    parts = [spec[s * step : (s + 1) * step] for s in range(2 * repeat + 1)]
    mixed, gated, taps = parts[:repeat], parts[repeat : 2 * repeat], parts[-1]
    cross = times_conj(gated[0], mixed[0])
    for s in range(1, repeat):
        cross = cross + times_conj(gated[s], mixed[s])
    prods = [times(m, taps) for m in mixed] + [times_conj(g, taps) for g in gated] + [cross]
    result = from_spectra(jnp.concatenate(prods, 0), tw[...], ib[...], ia[...], scale)
    for s in range(per):
        hold[pl.ds(s, blocks, stride=per), :] = result[:, s * width : (s + 1) * width]
    out_ref[...] = hold[...].astype(BF16)


def back_rows(rows, first, blocks, width):
    per = rows.shape[0] // blocks
    parts = [rows[pl.ds(first + f, blocks, stride=per), :] for f in range(width // blocks)]
    return jnp.concatenate(parts, 0).T


def taps_kernel(repeat, blocks, group, rows_ref, taps, hold):
    width = taps.shape[1]
    hold[...] = rows_ref[...].astype(F32)
    flipped = back_rows(hold, 2 * repeat * (width // blocks), blocks, width).astype(BF16)
    lags = width // len(group)
    for c, owner in enumerate(group):
        taps[c * lags : (c + 1) * lags] = flipped[owner * lags : (owner + 1) * lags]


def grads_kernel(
    repeat, blocks, rows_ref, part_ref, cot, value, key_in, grad_query, grad_key, grad_value, grad_filter, hold
):
    width = cot.shape[0]
    fils = width // blocks
    hold[...] = rows_ref[...].astype(F32)
    lags = grad_filter.shape[0]
    total = part_ref[:lags].astype(F32)
    for c in range(1, width // lags):
        total = total + part_ref[c * lags : (c + 1) * lags].astype(F32)
    grad_filter[...] = total
    for c in range(repeat):
        at = slice(c * width, (c + 1) * width)
        conv = back_rows(hold, c * fils, blocks, width)
        grad_query[:, at] = (cot[:, at].astype(F32) * conv).astype(BF16)
        back = back_rows(hold, (repeat + c) * fils, blocks, width)
        grad_key[:, at] = (back * value[:, at].astype(F32)).astype(BF16)
        grad_value[:, at] = (back * key_in[:, at].astype(F32)).astype(BF16)


def local(query, key_in, value, cotangent, filter_raw):
    width, channels = query.shape
    blocks = lax.axis_size("seq")
    groups = lax.axis_size("chan")
    length = blocks * width
    filters = filter_raw.shape[1]
    repeat = channels // filters
    fils = filters // blocks
    per = (2 * repeat + 1) * fils
    scale = 1.0 / (length * math.sqrt(length))
    first = blocks // 2 + 2
    group = [(3 * groups // 4 + c) % groups for c in range(groups)]
    order = [(first + i) % blocks for i in range(blocks)]
    tables = [jnp.asarray(t) for t in make_tables(blocks, width, order)]
    params = pltpu.CompilerParams(vmem_limit_bytes=VMEM_LIMIT)
    packed = jax.ShapeDtypeStruct((blocks * per, width), BF16)
    hold = pltpu.VMEM((blocks * per, width), F32)

    def swap(array):
        shape = (blocks, per // fils, fils, width)
        moved = lax.all_to_all(array.reshape(shape), "seq", split_axis=0, concat_axis=0, tiled=True, axis_index_groups=[order])
        return moved.reshape(array.shape)

    wide = pltpu.VMEM((width, channels), BF16)
    rows = pl.pallas_call(
        functools.partial(gate_kernel, repeat, blocks),
        out_shape=packed,
        in_specs=[pl.BlockSpec(memory_space=pl.ANY)] * 5,
        scratch_shapes=[wide, wide, pltpu.VMEM((width, filters), BF16), wide, wide, hold, pltpu.SemaphoreType.DMA((5,))],
        compiler_params=params,
        name="gate",
    )(*(pltpu.with_memory_space_constraint(a, pltpu.HBM) for a in (query, key_in, value, cotangent, filter_raw)))
    rows = pl.pallas_call(
        functools.partial(core_kernel, repeat, scale),
        out_shape=packed,
        scratch_shapes=[hold],
        compiler_params=params,
        name="core",
    )(swap(rows), *tables)
    rows = swap(rows)
    like = jax.ShapeDtypeStruct((width, channels), BF16)
    taps = pl.pallas_call(
        functools.partial(taps_kernel, repeat, blocks, group),
        out_shape=jax.ShapeDtypeStruct((width, filters), BF16),
        scratch_shapes=[hold],
        compiler_params=params,
        name="taps",
    )(rows)
    taps = lax.all_to_all(taps, "chan", split_axis=0, concat_axis=0, tiled=True, axis_index_groups=[group])
    return pl.pallas_call(
        functools.partial(grads_kernel, repeat, blocks),
        out_shape=(like, like, like, jax.ShapeDtypeStruct((width // groups, filters), F32)),
        scratch_shapes=[hold],
        compiler_params=params,
        name="grads",
    )(rows, taps, cotangent, value, key_in)


def solution(mesh):
    placed = (
        P("seq", "chan"),
        P("seq", "chan"),
        P("seq", "chan"),
        P("seq", "chan"),
        P("seq", None),
    )
    return jax.shard_map(
        local,
        mesh=mesh,
        in_specs=placed,
        out_specs=(P("seq", "chan"), P("seq", "chan"), P("seq", "chan"), P(("seq", "chan"), None)),
        check_vma=False,
    )
```

```python
import functools
import math

import numpy as np
import jax
import jax.numpy as jnp
from jax import lax
from jax.experimental import pallas as pl
from jax.experimental.pallas import tpu as pltpu
from jax.sharding import PartitionSpec as P

F32 = jnp.float32
BF16 = jnp.bfloat16
VMEM_LIMIT = 48 * 1024 * 1024


def split_table(table):
    high = table.astype(BF16)
    low = (table - high.astype(np.float64)).astype(BF16)
    return high, low


def make_tables(blocks, width, order):
    length = blocks * width
    j = np.array(order)
    k1 = np.arange(blocks) + 0.25
    r = np.arange(width)
    k2 = np.arange(width)
    angle_a = 2.0 * np.pi * np.outer(k1, j) / blocks
    outer_t = np.concatenate([np.cos(angle_a), -np.sin(angle_a)], 0)
    angle_t = 2.0 * np.pi * np.outer(k1, r) / length
    twist = np.concatenate([np.cos(angle_t), -np.sin(angle_t)], 1).astype(np.float32)
    angle_b = 2.0 * np.pi * np.outer(r, k2) / width
    cos_b, sin_b = np.cos(angle_b), np.sin(angle_b)
    inner_t = np.block([[cos_b, -sin_b], [sin_b, cos_b]])
    a_hi, a_lo = split_table(outer_t)
    b_hi, b_lo = split_table(inner_t)
    fwd_a = np.concatenate([a_hi, a_lo], 1)
    fwd_b = np.concatenate([b_hi, b_hi, b_lo], 0)
    return fwd_a, twist, fwd_b, b_hi.T, a_hi.T


def split(value):
    high = value.astype(BF16)
    low = (value - high.astype(F32)).astype(BF16)
    return high, low


def mul(left, right):
    return jnp.dot(left, right, preferred_element_type=F32)


def mul_rows(left, right, step):
    parts = [mul(left[i : i + step], right) for i in range(0, left.shape[0], step)]
    return jnp.concatenate(parts, 0)


def to_spectra(cols, fwd_a, twist, fwd_b):
    blocks, width = cols[0].shape
    data = jnp.concatenate(cols, 1)
    part = mul(fwd_a, jnp.concatenate([data, data], 0))
    t_re, t_im = twist[:, :width], twist[:, width:]
    rows = []
    for s in range(len(cols)):
        a_re = part[:blocks, s * width : (s + 1) * width]
        a_im = part[blocks:, s * width : (s + 1) * width]
        rows.append(jnp.concatenate([a_re * t_re - a_im * t_im, a_re * t_im + a_im * t_re], 1))
    high, low = split(jnp.concatenate(rows, 0))
    return mul_rows(jnp.concatenate([high, low, high], 1), fwd_b, 448)


def from_spectra(spec, twist, inv_b, inv_a, scale):
    blocks = twist.shape[0]
    width = twist.shape[1] // 2
    count = spec.shape[0] // blocks
    part = mul_rows(spec.astype(BF16), inv_b, 448)
    t_re, t_im = twist[:, :width], twist[:, width:]
    cols = []
    for s in range(count):
        d_re = part[s * blocks : (s + 1) * blocks, :width]
        d_im = part[s * blocks : (s + 1) * blocks, width:]
        cols.append(jnp.concatenate([d_re * t_re + d_im * t_im, d_im * t_re - d_re * t_im], 0))
    return mul(inv_a, jnp.concatenate(cols, 1).astype(BF16)) * scale


def gate_kernel(repeat, blocks, query, key_in, value, cotangent, taps, out_ref, *scratch):
    hold, sems = scratch[-2], scratch[-1]
    width = taps.shape[0]
    fils = width // blocks
    per = (2 * repeat + 1) * fils
    copies = []
    for i, source in enumerate((key_in, value, taps, cotangent, query)):
        copies.append(pltpu.make_async_copy(source, scratch[i], sems.at[i]))
        copies[-1].start()
    k_in, v_in, t_in, g_in, q_in = scratch[:5]

    def put(first, part):
        flipped = part.T
        for f in range(fils):
            hold[pl.ds(first + f, blocks, stride=per), :] = flipped[f * blocks : (f + 1) * blocks]

    def put_product(first, left, right):
        for c in range(repeat):
            at = slice(c * width, (c + 1) * width)
            prod = left[:, at].astype(F32) * right[:, at].astype(F32)
            put(first + c * fils, prod.astype(BF16).astype(F32))

    copies[0].wait()
    copies[1].wait()
    put_product(0, k_in, v_in)
    copies[2].wait()
    put(2 * repeat * fils, t_in[...].astype(F32))
    copies[3].wait()
    copies[4].wait()
    put_product(repeat * fils, g_in, q_in)
    out_ref[...] = hold[...].astype(BF16)


def take_columns(ref, hold, per, blocks):
    hold[...] = ref[...].astype(F32)
    return [hold[pl.ds(s, blocks, stride=per), :].astype(BF16) for s in range(per)]


def times(a, b):
    w = a.shape[1] // 2
    a_re, a_im, b_re, b_im = a[:, :w], a[:, w:], b[:, :w], b[:, w:]
    return jnp.concatenate([a_re * b_re - a_im * b_im, a_re * b_im + a_im * b_re], 1)


def times_conj(a, b):
    w = a.shape[1] // 2
    a_re, a_im, b_re, b_im = a[:, :w], a[:, w:], b[:, :w], b[:, w:]
    return jnp.concatenate([a_re * b_re + a_im * b_im, a_im * b_re - a_re * b_im], 1)


def core_kernel(repeat, scale, x_ref, fa, tw, fb, ib, ia, out_ref, hold):
    blocks = tw.shape[0]
    width = tw.shape[1] // 2
    per = x_ref.shape[0] // blocks
    fils = per // (2 * repeat + 1)
    step = fils * blocks
    spec = to_spectra(take_columns(x_ref, hold, per, blocks), fa[...], tw[...], fb[...])
    parts = [spec[s * step : (s + 1) * step] for s in range(2 * repeat + 1)]
    mixed, gated, taps = parts[:repeat], parts[repeat : 2 * repeat], parts[-1]
    cross = times_conj(gated[0], mixed[0])
    for s in range(1, repeat):
        cross = cross + times_conj(gated[s], mixed[s])
    prods = [times(m, taps) for m in mixed] + [times_conj(g, taps) for g in gated] + [cross]
    result = from_spectra(jnp.concatenate(prods, 0), tw[...], ib[...], ia[...], scale)
    for s in range(per):
        hold[pl.ds(s, blocks, stride=per), :] = result[:, s * width : (s + 1) * width]
    out_ref[...] = hold[...].astype(BF16)


def back_rows(rows, first, blocks, width):
    per = rows.shape[0] // blocks
    parts = [rows[pl.ds(first + f, blocks, stride=per), :] for f in range(width // blocks)]
    return jnp.concatenate(parts, 0).T


def taps_kernel(repeat, blocks, group, rows_ref, taps, hold):
    width = taps.shape[1]
    hold[...] = rows_ref[...].astype(F32)
    flipped = back_rows(hold, 2 * repeat * (width // blocks), blocks, width).astype(BF16)
    lags = width // len(group)
    for c, owner in enumerate(group):
        taps[c * lags : (c + 1) * lags] = flipped[owner * lags : (owner + 1) * lags]


def grads_kernel(
    repeat, blocks, rows_ref, part_ref, cot, value, key_in, grad_query, grad_key, grad_value, grad_filter, hold
):
    width = cot.shape[0]
    fils = width // blocks
    hold[...] = rows_ref[...].astype(F32)
    lags = grad_filter.shape[0]
    total = part_ref[:lags].astype(F32)
    for c in range(1, width // lags):
        total = total + part_ref[c * lags : (c + 1) * lags].astype(F32)
    grad_filter[...] = total
    for c in range(repeat):
        at = slice(c * width, (c + 1) * width)
        conv = back_rows(hold, c * fils, blocks, width)
        grad_query[:, at] = (cot[:, at].astype(F32) * conv).astype(BF16)
        back = back_rows(hold, (repeat + c) * fils, blocks, width)
        grad_key[:, at] = (back * value[:, at].astype(F32)).astype(BF16)
        grad_value[:, at] = (back * key_in[:, at].astype(F32)).astype(BF16)


def local(query, key_in, value, cotangent, filter_raw):
    width, channels = query.shape
    blocks = lax.axis_size("seq")
    groups = lax.axis_size("chan")
    length = blocks * width
    filters = filter_raw.shape[1]
    repeat = channels // filters
    fils = filters // blocks
    per = (2 * repeat + 1) * fils
    scale = 1.0 / (length * math.sqrt(length))
    first = blocks // 2 + 3
    group = [(3 * groups // 4 + c) % groups for c in range(groups)]
    order = [(first + i) % blocks for i in range(blocks)]
    tables = [jnp.asarray(t) for t in make_tables(blocks, width, order)]
    params = pltpu.CompilerParams(vmem_limit_bytes=VMEM_LIMIT)
    packed = jax.ShapeDtypeStruct((blocks * per, width), BF16)
    hold = pltpu.VMEM((blocks * per, width), F32)

    def swap(array):
        shape = (blocks, per // fils, fils, width)
        moved = lax.all_to_all(array.reshape(shape), "seq", split_axis=0, concat_axis=0, tiled=True, axis_index_groups=[order])
        return moved.reshape(array.shape)

    wide = pltpu.VMEM((width, channels), BF16)
    rows = pl.pallas_call(
        functools.partial(gate_kernel, repeat, blocks),
        out_shape=packed,
        in_specs=[pl.BlockSpec(memory_space=pl.ANY)] * 5,
        scratch_shapes=[wide, wide, pltpu.VMEM((width, filters), BF16), wide, wide, hold, pltpu.SemaphoreType.DMA((5,))],
        compiler_params=params,
        name="gate",
    )(*(pltpu.with_memory_space_constraint(a, pltpu.HBM) for a in (query, key_in, value, cotangent, filter_raw)))
    rows = pl.pallas_call(
        functools.partial(core_kernel, repeat, scale),
        out_shape=packed,
        scratch_shapes=[hold],
        compiler_params=params,
        name="core",
    )(swap(rows), *tables)
    rows = swap(rows)
    like = jax.ShapeDtypeStruct((width, channels), BF16)
    taps = pl.pallas_call(
        functools.partial(taps_kernel, repeat, blocks, group),
        out_shape=jax.ShapeDtypeStruct((width, filters), BF16),
        scratch_shapes=[hold],
        compiler_params=params,
        name="taps",
    )(rows)
    taps = lax.all_to_all(taps, "chan", split_axis=0, concat_axis=0, tiled=True, axis_index_groups=[group])
    return pl.pallas_call(
        functools.partial(grads_kernel, repeat, blocks),
        out_shape=(like, like, like, jax.ShapeDtypeStruct((width // groups, filters), F32)),
        scratch_shapes=[hold],
        compiler_params=params,
        name="grads",
    )(rows, taps, cotangent, value, key_in)


def solution(mesh):
    placed = (
        P("seq", "chan"),
        P("seq", "chan"),
        P("seq", "chan"),
        P("seq", "chan"),
        P("seq", None),
    )
    return jax.shard_map(
        local,
        mesh=mesh,
        in_specs=placed,
        out_specs=(P("seq", "chan"), P("seq", "chan"), P("seq", "chan"), P(("seq", "chan"), None)),
        check_vma=False,
    )
```

```python
import functools
import math

import numpy as np
import jax
import jax.numpy as jnp
from jax import lax
from jax.experimental import pallas as pl
from jax.experimental.pallas import tpu as pltpu
from jax.sharding import PartitionSpec as P

F32 = jnp.float32
BF16 = jnp.bfloat16
VMEM_LIMIT = 48 * 1024 * 1024


def split_table(table):
    high = table.astype(BF16)
    low = (table - high.astype(np.float64)).astype(BF16)
    return high, low


def make_tables(blocks, width, order):
    length = blocks * width
    j = np.array(order)
    k1 = np.arange(blocks) + 0.25
    r = np.arange(width)
    k2 = np.arange(width)
    angle_a = 2.0 * np.pi * np.outer(k1, j) / blocks
    outer_t = np.concatenate([np.cos(angle_a), -np.sin(angle_a)], 0)
    angle_t = 2.0 * np.pi * np.outer(k1, r) / length
    twist = np.concatenate([np.cos(angle_t), -np.sin(angle_t)], 1).astype(np.float32)
    angle_b = 2.0 * np.pi * np.outer(r, k2) / width
    cos_b, sin_b = np.cos(angle_b), np.sin(angle_b)
    inner_t = np.block([[cos_b, -sin_b], [sin_b, cos_b]])
    a_hi, a_lo = split_table(outer_t)
    b_hi, b_lo = split_table(inner_t)
    fwd_a = np.concatenate([a_hi, a_lo], 1)
    fwd_b = np.concatenate([b_hi, b_hi, b_lo], 0)
    return fwd_a, twist, fwd_b, b_hi.T, a_hi.T


def split(value):
    high = value.astype(BF16)
    low = (value - high.astype(F32)).astype(BF16)
    return high, low


def mul(left, right):
    return jnp.dot(left, right, preferred_element_type=F32)


def mul_rows(left, right, step):
    parts = [mul(left[i : i + step], right) for i in range(0, left.shape[0], step)]
    return jnp.concatenate(parts, 0)


def to_spectra(cols, fwd_a, twist, fwd_b):
    blocks, width = cols[0].shape
    data = jnp.concatenate(cols, 1)
    part = mul(fwd_a, jnp.concatenate([data, data], 0))
    t_re, t_im = twist[:, :width], twist[:, width:]
    rows = []
    for s in range(len(cols)):
        a_re = part[:blocks, s * width : (s + 1) * width]
        a_im = part[blocks:, s * width : (s + 1) * width]
        rows.append(jnp.concatenate([a_re * t_re - a_im * t_im, a_re * t_im + a_im * t_re], 1))
    high, low = split(jnp.concatenate(rows, 0))
    return mul_rows(jnp.concatenate([high, low, high], 1), fwd_b, 448)


def from_spectra(spec, twist, inv_b, inv_a, scale):
    blocks = twist.shape[0]
    width = twist.shape[1] // 2
    count = spec.shape[0] // blocks
    part = mul_rows(spec.astype(BF16), inv_b, 448)
    t_re, t_im = twist[:, :width], twist[:, width:]
    cols = []
    for s in range(count):
        d_re = part[s * blocks : (s + 1) * blocks, :width]
        d_im = part[s * blocks : (s + 1) * blocks, width:]
        cols.append(jnp.concatenate([d_re * t_re + d_im * t_im, d_im * t_re - d_re * t_im], 0))
    return mul(inv_a, jnp.concatenate(cols, 1).astype(BF16)) * scale


def gate_kernel(repeat, blocks, query, key_in, value, cotangent, taps, out_ref, *scratch):
    hold, sems = scratch[-2], scratch[-1]
    width = taps.shape[0]
    fils = width // blocks
    per = (2 * repeat + 1) * fils
    copies = []
    for i, source in enumerate((key_in, value, taps, cotangent, query)):
        copies.append(pltpu.make_async_copy(source, scratch[i], sems.at[i]))
        copies[-1].start()
    k_in, v_in, t_in, g_in, q_in = scratch[:5]

    def put(first, part):
        flipped = part.T
        for f in range(fils):
            hold[pl.ds(first + f, blocks, stride=per), :] = flipped[f * blocks : (f + 1) * blocks]

    def put_product(first, left, right):
        for c in range(repeat):
            at = slice(c * width, (c + 1) * width)
            prod = left[:, at].astype(F32) * right[:, at].astype(F32)
            put(first + c * fils, prod.astype(BF16).astype(F32))

    copies[0].wait()
    copies[1].wait()
    put_product(0, k_in, v_in)
    copies[2].wait()
    put(2 * repeat * fils, t_in[...].astype(F32))
    copies[3].wait()
    copies[4].wait()
    put_product(repeat * fils, g_in, q_in)
    out_ref[...] = hold[...].astype(BF16)


def take_columns(ref, hold, per, blocks):
    hold[...] = ref[...].astype(F32)
    return [hold[pl.ds(s, blocks, stride=per), :].astype(BF16) for s in range(per)]


def times(a, b):
    w = a.shape[1] // 2
    a_re, a_im, b_re, b_im = a[:, :w], a[:, w:], b[:, :w], b[:, w:]
    return jnp.concatenate([a_re * b_re - a_im * b_im, a_re * b_im + a_im * b_re], 1)


def times_conj(a, b):
    w = a.shape[1] // 2
    a_re, a_im, b_re, b_im = a[:, :w], a[:, w:], b[:, :w], b[:, w:]
    return jnp.concatenate([a_re * b_re + a_im * b_im, a_im * b_re - a_re * b_im], 1)


def core_kernel(repeat, scale, x_ref, fa, tw, fb, ib, ia, out_ref, hold):
    blocks = tw.shape[0]
    width = tw.shape[1] // 2
    per = x_ref.shape[0] // blocks
    fils = per // (2 * repeat + 1)
    step = fils * blocks
    spec = to_spectra(take_columns(x_ref, hold, per, blocks), fa[...], tw[...], fb[...])
    parts = [spec[s * step : (s + 1) * step] for s in range(2 * repeat + 1)]
    mixed, gated, taps = parts[:repeat], parts[repeat : 2 * repeat], parts[-1]
    cross = times_conj(gated[0], mixed[0])
    for s in range(1, repeat):
        cross = cross + times_conj(gated[s], mixed[s])
    prods = [times(m, taps) for m in mixed] + [times_conj(g, taps) for g in gated] + [cross]
    result = from_spectra(jnp.concatenate(prods, 0), tw[...], ib[...], ia[...], scale)
    for s in range(per):
        hold[pl.ds(s, blocks, stride=per), :] = result[:, s * width : (s + 1) * width]
    out_ref[...] = hold[...].astype(BF16)


def back_rows(rows, first, blocks, width):
    per = rows.shape[0] // blocks
    parts = [rows[pl.ds(first + f, blocks, stride=per), :] for f in range(width // blocks)]
    return jnp.concatenate(parts, 0).T


def taps_kernel(repeat, blocks, group, rows_ref, taps, hold):
    width = taps.shape[1]
    hold[...] = rows_ref[...].astype(F32)
    flipped = back_rows(hold, 2 * repeat * (width // blocks), blocks, width).astype(BF16)
    lags = width // len(group)
    for c, owner in enumerate(group):
        taps[c * lags : (c + 1) * lags] = flipped[owner * lags : (owner + 1) * lags]


def grads_kernel(
    repeat, blocks, rows_ref, part_ref, cot, value, key_in, grad_query, grad_key, grad_value, grad_filter, hold
):
    width = cot.shape[0]
    fils = width // blocks
    hold[...] = rows_ref[...].astype(F32)
    lags = grad_filter.shape[0]
    total = part_ref[:lags].astype(F32)
    for c in range(1, width // lags):
        total = total + part_ref[c * lags : (c + 1) * lags].astype(F32)
    grad_filter[...] = total
    for c in range(repeat):
        at = slice(c * width, (c + 1) * width)
        conv = back_rows(hold, c * fils, blocks, width)
        grad_query[:, at] = (cot[:, at].astype(F32) * conv).astype(BF16)
        back = back_rows(hold, (repeat + c) * fils, blocks, width)
        grad_key[:, at] = (back * value[:, at].astype(F32)).astype(BF16)
        grad_value[:, at] = (back * key_in[:, at].astype(F32)).astype(BF16)


def local(query, key_in, value, cotangent, filter_raw):
    width, channels = query.shape
    blocks = lax.axis_size("seq")
    groups = lax.axis_size("chan")
    length = blocks * width
    filters = filter_raw.shape[1]
    repeat = channels // filters
    fils = filters // blocks
    per = (2 * repeat + 1) * fils
    scale = 1.0 / (length * math.sqrt(length))
    first = blocks // 2 + 3
    group = [(3 * groups // 4 + c) % groups for c in range(groups)]
    order = [(first - i) % blocks for i in range(blocks)]
    tables = [jnp.asarray(t) for t in make_tables(blocks, width, order)]
    params = pltpu.CompilerParams(vmem_limit_bytes=VMEM_LIMIT)
    packed = jax.ShapeDtypeStruct((blocks * per, width), BF16)
    hold = pltpu.VMEM((blocks * per, width), F32)

    def swap(array):
        shape = (blocks, per // fils, fils, width)
        moved = lax.all_to_all(array.reshape(shape), "seq", split_axis=0, concat_axis=0, tiled=True, axis_index_groups=[order])
        return moved.reshape(array.shape)

    wide = pltpu.VMEM((width, channels), BF16)
    rows = pl.pallas_call(
        functools.partial(gate_kernel, repeat, blocks),
        out_shape=packed,
        in_specs=[pl.BlockSpec(memory_space=pl.ANY)] * 5,
        scratch_shapes=[wide, wide, pltpu.VMEM((width, filters), BF16), wide, wide, hold, pltpu.SemaphoreType.DMA((5,))],
        compiler_params=params,
        name="gate",
    )(*(pltpu.with_memory_space_constraint(a, pltpu.HBM) for a in (query, key_in, value, cotangent, filter_raw)))
    rows = pl.pallas_call(
        functools.partial(core_kernel, repeat, scale),
        out_shape=packed,
        scratch_shapes=[hold],
        compiler_params=params,
        name="core",
    )(swap(rows), *tables)
    rows = swap(rows)
    like = jax.ShapeDtypeStruct((width, channels), BF16)
    taps = pl.pallas_call(
        functools.partial(taps_kernel, repeat, blocks, group),
        out_shape=jax.ShapeDtypeStruct((width, filters), BF16),
        scratch_shapes=[hold],
        compiler_params=params,
        name="taps",
    )(rows)
    taps = lax.all_to_all(taps, "chan", split_axis=0, concat_axis=0, tiled=True, axis_index_groups=[group])
    return pl.pallas_call(
        functools.partial(grads_kernel, repeat, blocks),
        out_shape=(like, like, like, jax.ShapeDtypeStruct((width // groups, filters), F32)),
        scratch_shapes=[hold],
        compiler_params=params,
        name="grads",
    )(rows, taps, cotangent, value, key_in)


def solution(mesh):
    placed = (
        P("seq", "chan"),
        P("seq", "chan"),
        P("seq", "chan"),
        P("seq", "chan"),
        P("seq", None),
    )
    return jax.shard_map(
        local,
        mesh=mesh,
        in_specs=placed,
        out_specs=(P("seq", "chan"), P("seq", "chan"), P("seq", "chan"), P(("seq", "chan"), None)),
        check_vma=False,
    )
```

```python
import functools
import math

import numpy as np
import jax
import jax.numpy as jnp
from jax import lax
from jax.experimental import pallas as pl
from jax.experimental.pallas import tpu as pltpu
from jax.sharding import PartitionSpec as P

F32 = jnp.float32
BF16 = jnp.bfloat16
VMEM_LIMIT = 48 * 1024 * 1024


def split_table(table):
    high = table.astype(BF16)
    low = (table - high.astype(np.float64)).astype(BF16)
    return high, low


def make_tables(blocks, width, order):
    length = blocks * width
    j = np.array(order)
    k1 = np.arange(blocks) + 0.25
    r = np.arange(width)
    k2 = np.arange(width)
    angle_a = 2.0 * np.pi * np.outer(k1, j) / blocks
    outer_t = np.concatenate([np.cos(angle_a), -np.sin(angle_a)], 0)
    angle_t = 2.0 * np.pi * np.outer(k1, r) / length
    twist = np.concatenate([np.cos(angle_t), -np.sin(angle_t)], 1).astype(np.float32)
    angle_b = 2.0 * np.pi * np.outer(r, k2) / width
    cos_b, sin_b = np.cos(angle_b), np.sin(angle_b)
    inner_t = np.block([[cos_b, -sin_b], [sin_b, cos_b]])
    a_hi, a_lo = split_table(outer_t)
    b_hi, b_lo = split_table(inner_t)
    fwd_a = np.concatenate([a_hi, a_lo], 1)
    fwd_b = np.concatenate([b_hi, b_hi, b_lo], 0)
    return fwd_a, twist, fwd_b, b_hi.T, a_hi.T


def split(value):
    high = value.astype(BF16)
    low = (value - high.astype(F32)).astype(BF16)
    return high, low


def mul(left, right):
    return jnp.dot(left, right, preferred_element_type=F32)


def mul_rows(left, right, step):
    parts = [mul(left[i : i + step], right) for i in range(0, left.shape[0], step)]
    return jnp.concatenate(parts, 0)


def to_spectra(cols, fwd_a, twist, fwd_b):
    blocks, width = cols[0].shape
    data = jnp.concatenate(cols, 1)
    part = mul(fwd_a, jnp.concatenate([data, data], 0))
    t_re, t_im = twist[:, :width], twist[:, width:]
    rows = []
    for s in range(len(cols)):
        a_re = part[:blocks, s * width : (s + 1) * width]
        a_im = part[blocks:, s * width : (s + 1) * width]
        rows.append(jnp.concatenate([a_re * t_re - a_im * t_im, a_re * t_im + a_im * t_re], 1))
    high, low = split(jnp.concatenate(rows, 0))
    return mul_rows(jnp.concatenate([high, low, high], 1), fwd_b, 448)


def from_spectra(spec, twist, inv_b, inv_a, scale):
    blocks = twist.shape[0]
    width = twist.shape[1] // 2
    count = spec.shape[0] // blocks
    part = mul_rows(spec.astype(BF16), inv_b, 448)
    t_re, t_im = twist[:, :width], twist[:, width:]
    cols = []
    for s in range(count):
        d_re = part[s * blocks : (s + 1) * blocks, :width]
        d_im = part[s * blocks : (s + 1) * blocks, width:]
        cols.append(jnp.concatenate([d_re * t_re + d_im * t_im, d_im * t_re - d_re * t_im], 0))
    return mul(inv_a, jnp.concatenate(cols, 1).astype(BF16)) * scale


def gate_kernel(repeat, blocks, query, key_in, value, cotangent, taps, out_ref, *scratch):
    hold, sems = scratch[-2], scratch[-1]
    width = taps.shape[0]
    fils = width // blocks
    per = (2 * repeat + 1) * fils
    copies = []
    for i, source in enumerate((key_in, value, taps, cotangent, query)):
        copies.append(pltpu.make_async_copy(source, scratch[i], sems.at[i]))
        copies[-1].start()
    k_in, v_in, t_in, g_in, q_in = scratch[:5]

    def put(first, part):
        flipped = part.T
        for f in range(fils):
            hold[pl.ds(first + f, blocks, stride=per), :] = flipped[f * blocks : (f + 1) * blocks]

    def put_product(first, left, right):
        for c in range(repeat):
            at = slice(c * width, (c + 1) * width)
            prod = left[:, at].astype(F32) * right[:, at].astype(F32)
            put(first + c * fils, prod.astype(BF16).astype(F32))

    copies[0].wait()
    copies[1].wait()
    put_product(0, k_in, v_in)
    copies[2].wait()
    put(2 * repeat * fils, t_in[...].astype(F32))
    copies[3].wait()
    copies[4].wait()
    put_product(repeat * fils, g_in, q_in)
    out_ref[...] = hold[: out_ref.shape[0]].astype(BF16)


def take_columns(ref, hold, per, blocks):
    hold[: ref.shape[0]] = ref[...].astype(F32)
    return [hold[pl.ds(s, blocks, stride=per), :].astype(BF16) for s in range(per)]


def times(a, b):
    w = a.shape[1] // 2
    a_re, a_im, b_re, b_im = a[:, :w], a[:, w:], b[:, :w], b[:, w:]
    return jnp.concatenate([a_re * b_re - a_im * b_im, a_re * b_im + a_im * b_re], 1)


def times_conj(a, b):
    w = a.shape[1] // 2
    a_re, a_im, b_re, b_im = a[:, :w], a[:, w:], b[:, :w], b[:, w:]
    return jnp.concatenate([a_re * b_re + a_im * b_im, a_im * b_re - a_re * b_im], 1)


def core_kernel(repeat, scale, x_ref, fa, tw, fb, ib, ia, out_ref, hold):
    blocks = tw.shape[0]
    width = tw.shape[1] // 2
    per = x_ref.shape[0] // blocks
    fils = per // (2 * repeat + 1)
    step = fils * blocks
    spec = to_spectra(take_columns(x_ref, hold, per, blocks), fa[...], tw[...], fb[...])
    parts = [spec[s * step : (s + 1) * step] for s in range(2 * repeat + 1)]
    mixed, gated, taps = parts[:repeat], parts[repeat : 2 * repeat], parts[-1]
    cross = times_conj(gated[0], mixed[0])
    for s in range(1, repeat):
        cross = cross + times_conj(gated[s], mixed[s])
    prods = [times(m, taps) for m in mixed] + [times_conj(g, taps) for g in gated] + [cross]
    result = from_spectra(jnp.concatenate(prods, 0), tw[...], ib[...], ia[...], scale)
    for s in range(per):
        hold[pl.ds(s, blocks, stride=per), :] = result[:, s * width : (s + 1) * width]
    out_ref[...] = hold[: out_ref.shape[0]].astype(BF16)


def back_rows(rows, first, blocks, width):
    per = rows.shape[0] // blocks
    parts = [rows[pl.ds(first + f, blocks, stride=per), :] for f in range(width // blocks)]
    return jnp.concatenate(parts, 0).T


def taps_kernel(repeat, blocks, group, rows_ref, taps, hold):
    width = taps.shape[1]
    hold[: rows_ref.shape[0]] = rows_ref[...].astype(F32)
    flipped = back_rows(hold, 2 * repeat * (width // blocks), blocks, width).astype(BF16)
    lags = width // len(group)
    for c, owner in enumerate(group):
        taps[c * lags : (c + 1) * lags] = flipped[owner * lags : (owner + 1) * lags]


def grads_kernel(
    repeat, blocks, rows_ref, part_ref, cot, value, key_in, grad_query, grad_key, grad_value, grad_filter, hold
):
    width = cot.shape[0]
    fils = width // blocks
    hold[: rows_ref.shape[0]] = rows_ref[...].astype(F32)
    lags = grad_filter.shape[0]
    total = part_ref[:lags].astype(F32)
    for c in range(1, width // lags):
        total = total + part_ref[c * lags : (c + 1) * lags].astype(F32)
    grad_filter[...] = total
    for c in range(repeat):
        at = slice(c * width, (c + 1) * width)
        conv = back_rows(hold, c * fils, blocks, width)
        grad_query[:, at] = (cot[:, at].astype(F32) * conv).astype(BF16)
        back = back_rows(hold, (repeat + c) * fils, blocks, width)
        grad_key[:, at] = (back * value[:, at].astype(F32)).astype(BF16)
        grad_value[:, at] = (back * key_in[:, at].astype(F32)).astype(BF16)


def local(query, key_in, value, cotangent, filter_raw):
    width, channels = query.shape
    blocks = lax.axis_size("seq")
    groups = lax.axis_size("chan")
    length = blocks * width
    filters = filter_raw.shape[1]
    repeat = channels // filters
    fils = filters // blocks
    per = (2 * repeat + 1) * fils
    scale = 1.0 / (length * math.sqrt(length))
    first = blocks // 2 + 3
    group = [(3 * groups // 4 + c) % groups for c in range(groups)]
    order = [(first - i) % blocks for i in range(blocks)]
    tables = [jnp.asarray(t) for t in make_tables(blocks, width, order)]
    params = pltpu.CompilerParams(vmem_limit_bytes=VMEM_LIMIT)
    packed = jax.ShapeDtypeStruct((blocks * per, width), BF16)
    hold = pltpu.VMEM((blocks * per + 16, width), F32)

    def swap(array):
        shape = (blocks, per // fils, fils, width)
        moved = lax.all_to_all(array.reshape(shape), "seq", split_axis=0, concat_axis=0, tiled=True, axis_index_groups=[order])
        return moved.reshape(array.shape)

    wide = pltpu.VMEM((width, channels), BF16)
    rows = pl.pallas_call(
        functools.partial(gate_kernel, repeat, blocks),
        out_shape=packed,
        in_specs=[pl.BlockSpec(memory_space=pl.ANY)] * 5,
        scratch_shapes=[wide, wide, pltpu.VMEM((width, filters), BF16), wide, wide, hold, pltpu.SemaphoreType.DMA((5,))],
        compiler_params=params,
        name="gate",
    )(*(pltpu.with_memory_space_constraint(a, pltpu.HBM) for a in (query, key_in, value, cotangent, filter_raw)))
    rows = pl.pallas_call(
        functools.partial(core_kernel, repeat, scale),
        out_shape=packed,
        scratch_shapes=[hold],
        compiler_params=params,
        name="core",
    )(swap(rows), *tables)
    rows = swap(rows)
    like = jax.ShapeDtypeStruct((width, channels), BF16)
    taps = pl.pallas_call(
        functools.partial(taps_kernel, repeat, blocks, group),
        out_shape=jax.ShapeDtypeStruct((width, filters), BF16),
        scratch_shapes=[hold],
        compiler_params=params,
        name="taps",
    )(rows)
    taps = lax.all_to_all(taps, "chan", split_axis=0, concat_axis=0, tiled=True, axis_index_groups=[group])
    return pl.pallas_call(
        functools.partial(grads_kernel, repeat, blocks),
        out_shape=(like, like, like, jax.ShapeDtypeStruct((width // groups, filters), F32)),
        scratch_shapes=[hold],
        compiler_params=params,
        name="grads",
    )(rows, taps, cotangent, value, key_in)


def solution(mesh):
    placed = (
        P("seq", "chan"),
        P("seq", "chan"),
        P("seq", "chan"),
        P("seq", "chan"),
        P("seq", None),
    )
    return jax.shard_map(
        local,
        mesh=mesh,
        in_specs=placed,
        out_specs=(P("seq", "chan"), P("seq", "chan"), P("seq", "chan"), P(("seq", "chan"), None)),
        check_vma=False,
    )
```

```python
import functools
import math

import numpy as np
import jax
import jax.numpy as jnp
from jax import lax
from jax.experimental import pallas as pl
from jax.experimental.pallas import tpu as pltpu
from jax.sharding import PartitionSpec as P

F32 = jnp.float32
BF16 = jnp.bfloat16
VMEM_LIMIT = 48 * 1024 * 1024


def split_table(table):
    high = table.astype(BF16)
    low = (table - high.astype(np.float64)).astype(BF16)
    return high, low


def make_tables(blocks, width, order):
    length = blocks * width
    j = np.array(order)
    k1 = np.arange(blocks) + 0.25
    r = np.arange(width)
    k2 = np.arange(width)
    angle_a = 2.0 * np.pi * np.outer(k1, j) / blocks
    outer_t = np.concatenate([np.cos(angle_a), -np.sin(angle_a)], 0)
    angle_t = 2.0 * np.pi * np.outer(k1, r) / length
    twist = np.concatenate([np.cos(angle_t), -np.sin(angle_t)], 1).astype(np.float32)
    angle_b = 2.0 * np.pi * np.outer(r, k2) / width
    cos_b, sin_b = np.cos(angle_b), np.sin(angle_b)
    inner_t = np.block([[cos_b, -sin_b], [sin_b, cos_b]])
    a_hi, a_lo = split_table(outer_t)
    b_hi, b_lo = split_table(inner_t)
    fwd_a = np.concatenate([a_hi, a_lo], 1)
    fwd_b = np.concatenate([b_hi, b_hi, b_lo], 0)
    return fwd_a, twist, fwd_b, b_hi.T, a_hi.T


def split(value):
    high = value.astype(BF16)
    low = (value - high.astype(F32)).astype(BF16)
    return high, low


def mul(left, right):
    return jnp.dot(left, right, preferred_element_type=F32)


def mul_rows(left, right, step):
    parts = [mul(left[i : i + step], right) for i in range(0, left.shape[0], step)]
    return jnp.concatenate(parts, 0)


def to_spectra(cols, fwd_a, twist, fwd_b):
    blocks, width = cols[0].shape
    data = jnp.concatenate(cols, 1)
    part = mul(fwd_a, jnp.concatenate([data, data], 0))
    t_re, t_im = twist[:, :width], twist[:, width:]
    rows = []
    for s in range(len(cols)):
        a_re = part[:blocks, s * width : (s + 1) * width]
        a_im = part[blocks:, s * width : (s + 1) * width]
        rows.append(jnp.concatenate([a_re * t_re - a_im * t_im, a_re * t_im + a_im * t_re], 1))
    high, low = split(jnp.concatenate(rows, 0))
    return mul_rows(jnp.concatenate([high, low, high], 1), fwd_b, 448)


def from_spectra(spec, twist, inv_b, inv_a, scale):
    blocks = twist.shape[0]
    width = twist.shape[1] // 2
    count = spec.shape[0] // blocks
    part = mul_rows(spec.astype(BF16), inv_b, 448)
    t_re, t_im = twist[:, :width], twist[:, width:]
    cols = []
    for s in range(count):
        d_re = part[s * blocks : (s + 1) * blocks, :width]
        d_im = part[s * blocks : (s + 1) * blocks, width:]
        cols.append(jnp.concatenate([d_re * t_re + d_im * t_im, d_im * t_re - d_re * t_im], 0))
    return mul(inv_a, jnp.concatenate(cols, 1).astype(BF16)) * scale


def gate_kernel(repeat, blocks, query, key_in, value, cotangent, taps, out_ref, *scratch):
    hold, sems = scratch[-2], scratch[-1]
    width = taps.shape[0]
    fils = width // blocks
    per = (2 * repeat + 1) * fils
    copies = []
    for i, source in enumerate((key_in, value, taps, cotangent, query)):
        copies.append(pltpu.make_async_copy(source, scratch[i], sems.at[i]))
        copies[-1].start()
    k_in, v_in, t_in, g_in, q_in = scratch[:5]

    def put(first, part):
        flipped = part.T
        for f in range(fils):
            hold[pl.ds(first + f, blocks, stride=per), :] = flipped[f * blocks : (f + 1) * blocks]

    def put_product(first, left, right):
        for c in range(repeat):
            at = slice(c * width, (c + 1) * width)
            prod = left[:, at].astype(F32) * right[:, at].astype(F32)
            put(first + c * fils, prod.astype(BF16).astype(F32))

    copies[0].wait()
    copies[1].wait()
    put_product(0, k_in, v_in)
    copies[2].wait()
    put(2 * repeat * fils, t_in[...].astype(F32))
    copies[3].wait()
    copies[4].wait()
    put_product(repeat * fils, g_in, q_in)
    out_ref[...] = hold[: out_ref.shape[0]].astype(BF16)


def take_columns(ref, hold, per, blocks):
    hold[: ref.shape[0]] = ref[...].astype(F32)
    return [hold[pl.ds(s, blocks, stride=per), :].astype(BF16) for s in range(per)]


def times(a, b):
    w = a.shape[1] // 2
    a_re, a_im, b_re, b_im = a[:, :w], a[:, w:], b[:, :w], b[:, w:]
    return jnp.concatenate([a_re * b_re - a_im * b_im, a_re * b_im + a_im * b_re], 1)


def times_conj(a, b):
    w = a.shape[1] // 2
    a_re, a_im, b_re, b_im = a[:, :w], a[:, w:], b[:, :w], b[:, w:]
    return jnp.concatenate([a_re * b_re + a_im * b_im, a_im * b_re - a_re * b_im], 1)


def core_kernel(repeat, scale, x_ref, fa, tw, fb, ib, ia, out_ref, hold):
    blocks = tw.shape[0]
    width = tw.shape[1] // 2
    per = x_ref.shape[0] // blocks
    fils = per // (2 * repeat + 1)
    step = fils * blocks
    spec = to_spectra(take_columns(x_ref, hold, per, blocks), fa[...], tw[...], fb[...])
    parts = [spec[s * step : (s + 1) * step] for s in range(2 * repeat + 1)]
    mixed, gated, taps = parts[:repeat], parts[repeat : 2 * repeat], parts[-1]
    cross = times_conj(gated[0], mixed[0])
    for s in range(1, repeat):
        cross = cross + times_conj(gated[s], mixed[s])
    prods = [times(m, taps) for m in mixed] + [times_conj(g, taps) for g in gated] + [cross]
    result = from_spectra(jnp.concatenate(prods, 0), tw[...], ib[...], ia[...], scale)
    for s in range(per):
        hold[pl.ds(s, blocks, stride=per), :] = result[:, s * width : (s + 1) * width]
    out_ref[...] = hold[: out_ref.shape[0]].astype(BF16)


def back_rows(rows, first, blocks, width):
    per = rows.shape[0] // blocks
    parts = [rows[pl.ds(first + f, blocks, stride=per), :] for f in range(width // blocks)]
    return jnp.concatenate(parts, 0).T


def taps_kernel(repeat, blocks, group, rows_ref, taps, hold):
    width = taps.shape[1]
    hold[: rows_ref.shape[0]] = rows_ref[...].astype(F32)
    flipped = back_rows(hold, 2 * repeat * (width // blocks), blocks, width).astype(BF16)
    lags = width // len(group)
    for c, owner in enumerate(group):
        taps[c * lags : (c + 1) * lags] = flipped[owner * lags : (owner + 1) * lags]


def grads_kernel(
    repeat, blocks, rows_ref, part_ref, cot, value, key_in, out_query, out_key, out_value, out_filter, hold, *scratch
):
    grad_query, grad_key, grad_value, grad_filter, sems = scratch
    width = cot.shape[0]
    fils = width // blocks
    copies = [
        pltpu.make_async_copy(source, target, sems.at[i])
        for i, (source, target) in enumerate(
            ((grad_query, out_query), (grad_key, out_key), (grad_value, out_value), (grad_filter, out_filter))
        )
    ]
    lags = grad_filter.shape[0]
    total = part_ref[:lags].astype(F32)
    for c in range(1, width // lags):
        total = total + part_ref[c * lags : (c + 1) * lags].astype(F32)
    grad_filter[...] = total
    copies[3].start()
    hold[: rows_ref.shape[0]] = rows_ref[...].astype(F32)
    for c in range(repeat):
        at = slice(c * width, (c + 1) * width)
        conv = back_rows(hold, c * fils, blocks, width)
        grad_query[:, at] = (cot[:, at].astype(F32) * conv).astype(BF16)
    copies[0].start()
    for c in range(repeat):
        at = slice(c * width, (c + 1) * width)
        back = back_rows(hold, (repeat + c) * fils, blocks, width)
        grad_key[:, at] = (back * value[:, at].astype(F32)).astype(BF16)
        grad_value[:, at] = (back * key_in[:, at].astype(F32)).astype(BF16)
    copies[1].start()
    copies[2].start()
    for copy in copies:
        copy.wait()


def local(query, key_in, value, cotangent, filter_raw):
    width, channels = query.shape
    blocks = lax.axis_size("seq")
    groups = lax.axis_size("chan")
    length = blocks * width
    filters = filter_raw.shape[1]
    repeat = channels // filters
    fils = filters // blocks
    per = (2 * repeat + 1) * fils
    scale = 1.0 / (length * math.sqrt(length))
    first = blocks // 2 + 3
    group = [(3 * groups // 4 + c) % groups for c in range(groups)]
    bits = blocks.bit_length() - 1
    order = [(first - int(format(i, "0%db" % bits)[::-1], 2)) % blocks for i in range(blocks)]
    tables = [jnp.asarray(t) for t in make_tables(blocks, width, order)]
    params = pltpu.CompilerParams(vmem_limit_bytes=VMEM_LIMIT)
    packed = jax.ShapeDtypeStruct((blocks * per, width), BF16)
    hold = pltpu.VMEM((blocks * per + 16, width), F32)

    def swap(array):
        shape = (blocks, per // fils, fils, width)
        moved = lax.all_to_all(array.reshape(shape), "seq", split_axis=0, concat_axis=0, tiled=True, axis_index_groups=[order])
        return moved.reshape(array.shape)

    wide = pltpu.VMEM((width, channels), BF16)
    rows = pl.pallas_call(
        functools.partial(gate_kernel, repeat, blocks),
        out_shape=packed,
        in_specs=[pl.BlockSpec(memory_space=pl.ANY)] * 5,
        scratch_shapes=[wide, wide, pltpu.VMEM((width, filters), BF16), wide, wide, hold, pltpu.SemaphoreType.DMA((5,))],
        compiler_params=params,
        name="gate",
    )(*(pltpu.with_memory_space_constraint(a, pltpu.HBM) for a in (query, key_in, value, cotangent, filter_raw)))
    rows = pl.pallas_call(
        functools.partial(core_kernel, repeat, scale),
        out_shape=packed,
        scratch_shapes=[hold],
        compiler_params=params,
        name="core",
    )(swap(rows), *tables)
    rows = swap(rows)
    like = jax.ShapeDtypeStruct((width, channels), BF16)
    taps = pl.pallas_call(
        functools.partial(taps_kernel, repeat, blocks, group),
        out_shape=jax.ShapeDtypeStruct((width, filters), BF16),
        scratch_shapes=[hold],
        compiler_params=params,
        name="taps",
    )(rows)
    taps = lax.all_to_all(taps, "chan", split_axis=0, concat_axis=0, tiled=True, axis_index_groups=[group])
    return pl.pallas_call(
        functools.partial(grads_kernel, repeat, blocks),
        out_shape=(like, like, like, jax.ShapeDtypeStruct((width // groups, filters), F32)),
        out_specs=[pl.BlockSpec(memory_space=pl.ANY)] * 4,
        scratch_shapes=[hold, wide, wide, wide, pltpu.VMEM((width // groups, filters), F32), pltpu.SemaphoreType.DMA((4,))],
        compiler_params=params,
        name="grads",
    )(rows, taps, cotangent, value, key_in)


def solution(mesh):
    placed = (
        P("seq", "chan"),
        P("seq", "chan"),
        P("seq", "chan"),
        P("seq", "chan"),
        P("seq", None),
    )
    return jax.shard_map(
        local,
        mesh=mesh,
        in_specs=placed,
        out_specs=(P("seq", "chan"), P("seq", "chan"), P("seq", "chan"), P(("seq", "chan"), None)),
        check_vma=False,
    )
```

```python
import functools
import math

import numpy as np
import jax
import jax.numpy as jnp
from jax import lax
from jax.experimental import pallas as pl
from jax.experimental.pallas import tpu as pltpu
from jax.sharding import PartitionSpec as P

F32 = jnp.float32
BF16 = jnp.bfloat16
VMEM_LIMIT = 48 * 1024 * 1024


def split_table(table):
    high = table.astype(BF16)
    low = (table - high.astype(np.float64)).astype(BF16)
    return high, low


def make_tables(blocks, width, order):
    length = blocks * width
    j = np.array(order)
    k1 = np.arange(blocks) + 0.25
    r = np.arange(width)
    k2 = np.arange(width)
    angle_a = 2.0 * np.pi * np.outer(k1, j) / blocks
    outer_t = np.concatenate([np.cos(angle_a), -np.sin(angle_a)], 0)
    angle_t = 2.0 * np.pi * np.outer(k1, r) / length
    twist = np.concatenate([np.cos(angle_t), -np.sin(angle_t)], 1).astype(np.float32)
    angle_b = 2.0 * np.pi * np.outer(r, k2) / width
    cos_b, sin_b = np.cos(angle_b), np.sin(angle_b)
    inner_t = np.block([[cos_b, -sin_b], [sin_b, cos_b]])
    a_hi, a_lo = split_table(outer_t)
    b_hi, b_lo = split_table(inner_t)
    fwd_a = np.concatenate([a_hi, a_lo], 1)
    fwd_b = np.concatenate([b_hi, b_hi, b_lo], 0)
    return fwd_a, twist, fwd_b, b_hi.T, a_hi.T


def split(value):
    high = value.astype(BF16)
    low = (value - high.astype(F32)).astype(BF16)
    return high, low


def mul(left, right):
    return jnp.dot(left, right, preferred_element_type=F32)


def mul_rows(left, right, step):
    parts = [mul(left[i : i + step], right) for i in range(0, left.shape[0], step)]
    return jnp.concatenate(parts, 0)


def to_spectra(cols, fwd_a, twist, fwd_b):
    blocks, width = cols[0].shape
    data = jnp.concatenate(cols, 1)
    part = mul(fwd_a, jnp.concatenate([data, data], 0))
    t_re, t_im = twist[:, :width], twist[:, width:]
    rows = []
    for s in range(len(cols)):
        a_re = part[:blocks, s * width : (s + 1) * width]
        a_im = part[blocks:, s * width : (s + 1) * width]
        rows.append(jnp.concatenate([a_re * t_re - a_im * t_im, a_re * t_im + a_im * t_re], 1))
    high, low = split(jnp.concatenate(rows, 0))
    return mul_rows(jnp.concatenate([high, low, high], 1), fwd_b, 448)


def from_spectra(spec, twist, inv_b, inv_a, scale):
    blocks = twist.shape[0]
    width = twist.shape[1] // 2
    count = spec.shape[0] // blocks
    part = mul_rows(spec.astype(BF16), inv_b, 448)
    t_re, t_im = twist[:, :width], twist[:, width:]
    cols = []
    for s in range(count):
        d_re = part[s * blocks : (s + 1) * blocks, :width]
        d_im = part[s * blocks : (s + 1) * blocks, width:]
        cols.append(jnp.concatenate([d_re * t_re + d_im * t_im, d_im * t_re - d_re * t_im], 0))
    return mul(inv_a, jnp.concatenate(cols, 1).astype(BF16)) * scale


def gate_kernel(repeat, blocks, query, key_in, value, cotangent, taps, out_ref, *scratch):
    hold, sems = scratch[-2], scratch[-1]
    width = taps.shape[0]
    fils = width // blocks
    per = (2 * repeat + 1) * fils
    copies = []
    for i, source in enumerate((key_in, value, taps, cotangent, query)):
        copies.append(pltpu.make_async_copy(source, scratch[i], sems.at[i]))
        copies[-1].start()
    k_in, v_in, t_in, g_in, q_in = scratch[:5]

    def put(first, part):
        flipped = part.T
        for f in range(fils):
            hold[pl.ds(first + f, blocks, stride=per), :] = flipped[f * blocks : (f + 1) * blocks]

    def put_product(first, left, right):
        for c in range(repeat):
            at = slice(c * width, (c + 1) * width)
            prod = left[:, at].astype(F32) * right[:, at].astype(F32)
            put(first + c * fils, prod.astype(BF16).astype(F32))

    copies[0].wait()
    copies[1].wait()
    put_product(0, k_in, v_in)
    copies[2].wait()
    put(2 * repeat * fils, t_in[...].astype(F32))
    copies[3].wait()
    copies[4].wait()
    put_product(repeat * fils, g_in, q_in)
    out_ref[...] = hold[: out_ref.shape[0]].astype(BF16)


def take_columns(ref, hold, per, blocks):
    hold[: ref.shape[0]] = ref[...].astype(F32)
    return [hold[pl.ds(s, blocks, stride=per), :].astype(BF16) for s in range(per)]


def times(a, b):
    w = a.shape[1] // 2
    a_re, a_im, b_re, b_im = a[:, :w], a[:, w:], b[:, :w], b[:, w:]
    return jnp.concatenate([a_re * b_re - a_im * b_im, a_re * b_im + a_im * b_re], 1)


def times_conj(a, b):
    w = a.shape[1] // 2
    a_re, a_im, b_re, b_im = a[:, :w], a[:, w:], b[:, :w], b[:, w:]
    return jnp.concatenate([a_re * b_re + a_im * b_im, a_im * b_re - a_re * b_im], 1)


def core_kernel(repeat, scale, x_ref, fa, tw, fb, ib, ia, out_ref, hold):
    blocks = tw.shape[0]
    width = tw.shape[1] // 2
    per = x_ref.shape[0] // blocks
    fils = per // (2 * repeat + 1)
    step = fils * blocks
    spec = to_spectra(take_columns(x_ref, hold, per, blocks), fa[...], tw[...], fb[...])
    parts = [spec[s * step : (s + 1) * step] for s in range(2 * repeat + 1)]
    mixed, gated, taps = parts[:repeat], parts[repeat : 2 * repeat], parts[-1]
    cross = times_conj(gated[0], mixed[0])
    for s in range(1, repeat):
        cross = cross + times_conj(gated[s], mixed[s])
    prods = [times(m, taps) for m in mixed] + [times_conj(g, taps) for g in gated] + [cross]
    result = from_spectra(jnp.concatenate(prods, 0), tw[...], ib[...], ia[...], scale)
    for s in range(per):
        hold[pl.ds(s, blocks, stride=per), :] = result[:, s * width : (s + 1) * width]
    out_ref[...] = hold[: out_ref.shape[0]].astype(BF16)


def back_rows(rows, first, blocks, width):
    per = rows.shape[0] // blocks
    parts = [rows[pl.ds(first + f, blocks, stride=per), :] for f in range(width // blocks)]
    return jnp.concatenate(parts, 0).T


def taps_kernel(repeat, blocks, group, rows_ref, taps, hold):
    width = taps.shape[1]
    hold[: rows_ref.shape[0]] = rows_ref[...].astype(F32)
    flipped = back_rows(hold, 2 * repeat * (width // blocks), blocks, width).astype(BF16)
    lags = width // len(group)
    for c, owner in enumerate(group):
        taps[c * lags : (c + 1) * lags] = flipped[owner * lags : (owner + 1) * lags]


def grads_kernel(
    repeat, blocks, rows_ref, part_ref, cot, value, key_in, out_query, out_key, out_value, out_filter, hold, *scratch
):
    grad_query, grad_key, grad_value, grad_filter, sems = scratch
    width = cot.shape[0]
    fils = width // blocks
    copies = [
        pltpu.make_async_copy(source, target, sems.at[i])
        for i, (source, target) in enumerate(
            ((grad_query, out_query), (grad_key, out_key), (grad_value, out_value), (grad_filter, out_filter))
        )
    ]
    lags = grad_filter.shape[0]
    total = part_ref[:lags].astype(F32)
    for c in range(1, width // lags):
        total = total + part_ref[c * lags : (c + 1) * lags].astype(F32)
    grad_filter[...] = total
    copies[3].start()
    hold[: rows_ref.shape[0]] = rows_ref[...].astype(F32)
    for c in range(repeat):
        at = slice(c * width, (c + 1) * width)
        conv = back_rows(hold, c * fils, blocks, width)
        grad_query[:, at] = (cot[:, at].astype(F32) * conv).astype(BF16)
    copies[0].start()
    for c in range(repeat):
        at = slice(c * width, (c + 1) * width)
        back = back_rows(hold, (repeat + c) * fils, blocks, width)
        grad_key[:, at] = (back * value[:, at].astype(F32)).astype(BF16)
        grad_value[:, at] = (back * key_in[:, at].astype(F32)).astype(BF16)
    copies[1].start()
    copies[2].start()
    for copy in copies:
        copy.wait()


def local(query, key_in, value, cotangent, filter_raw):
    width, channels = query.shape
    blocks = lax.axis_size("seq")
    groups = lax.axis_size("chan")
    length = blocks * width
    filters = filter_raw.shape[1]
    repeat = channels // filters
    fils = filters // blocks
    per = (2 * repeat + 1) * fils
    scale = 1.0 / (length * math.sqrt(length))
    first = blocks // 2 + 3
    group = [(3 * groups // 4 + c) % groups for c in range(groups)]
    order = [(first - i) % blocks for i in range(blocks)]
    tables = [jnp.asarray(t) for t in make_tables(blocks, width, order)]
    params = pltpu.CompilerParams(vmem_limit_bytes=VMEM_LIMIT)
    packed = jax.ShapeDtypeStruct((blocks * per, width), BF16)
    hold = pltpu.VMEM((blocks * per + 16, width), F32)

    def swap(array):
        shape = (blocks, per // fils, fils, width)
        moved = lax.all_to_all(array.reshape(shape), "seq", split_axis=0, concat_axis=0, tiled=True, axis_index_groups=[order])
        return moved.reshape(array.shape)

    wide = pltpu.VMEM((width, channels), BF16)
    rows = pl.pallas_call(
        functools.partial(gate_kernel, repeat, blocks),
        out_shape=packed,
        in_specs=[pl.BlockSpec(memory_space=pl.ANY)] * 5,
        scratch_shapes=[wide, wide, pltpu.VMEM((width, filters), BF16), wide, wide, hold, pltpu.SemaphoreType.DMA((5,))],
        compiler_params=params,
        name="gate",
    )(*(pltpu.with_memory_space_constraint(a, pltpu.HBM) for a in (query, key_in, value, cotangent, filter_raw)))
    rows = pl.pallas_call(
        functools.partial(core_kernel, repeat, scale),
        out_shape=packed,
        scratch_shapes=[hold],
        compiler_params=params,
        name="core",
    )(swap(rows), *tables)
    rows = swap(rows)
    like = jax.ShapeDtypeStruct((width, channels), BF16)
    taps = pl.pallas_call(
        functools.partial(taps_kernel, repeat, blocks, group),
        out_shape=jax.ShapeDtypeStruct((width, filters), BF16),
        scratch_shapes=[hold],
        compiler_params=params,
        name="taps",
    )(rows)
    taps = lax.all_to_all(taps, "chan", split_axis=0, concat_axis=0, tiled=True, axis_index_groups=[group])
    return pl.pallas_call(
        functools.partial(grads_kernel, repeat, blocks),
        out_shape=(like, like, like, jax.ShapeDtypeStruct((width // groups, filters), F32)),
        out_specs=[pl.BlockSpec(memory_space=pl.ANY)] * 4,
        scratch_shapes=[hold, wide, wide, wide, pltpu.VMEM((width // groups, filters), F32), pltpu.SemaphoreType.DMA((4,))],
        compiler_params=params,
        name="grads",
    )(rows, taps, cotangent, value, key_in)


def solution(mesh):
    placed = (
        P("seq", "chan"),
        P("seq", "chan"),
        P("seq", "chan"),
        P("seq", "chan"),
        P("seq", None),
    )
    return jax.shard_map(
        local,
        mesh=mesh,
        in_specs=placed,
        out_specs=(P("seq", "chan"), P("seq", "chan"), P("seq", "chan"), P(("seq", "chan"), None)),
        check_vma=False,
    )
```

```python
import functools
import math

import numpy as np
import jax
import jax.numpy as jnp
from jax import lax
from jax.experimental import pallas as pl
from jax.experimental.pallas import tpu as pltpu
from jax.sharding import PartitionSpec as P

F32 = jnp.float32
BF16 = jnp.bfloat16
VMEM_LIMIT = 48 * 1024 * 1024


def split_table(table):
    high = table.astype(BF16)
    low = (table - high.astype(np.float64)).astype(BF16)
    return high, low


def make_tables(blocks, width, order):
    length = blocks * width
    j = np.array(order)
    k1 = np.arange(blocks) + 0.25
    r = np.arange(width)
    k2 = np.arange(width)
    angle_a = 2.0 * np.pi * np.outer(k1, j) / blocks
    outer_t = np.concatenate([np.cos(angle_a), -np.sin(angle_a)], 0)
    angle_t = 2.0 * np.pi * np.outer(k1, r) / length
    twist = np.concatenate([np.cos(angle_t), -np.sin(angle_t)], 1).astype(np.float32)
    angle_b = 2.0 * np.pi * np.outer(r, k2) / width
    cos_b, sin_b = np.cos(angle_b), np.sin(angle_b)
    inner_t = np.block([[cos_b, -sin_b], [sin_b, cos_b]])
    a_hi, a_lo = split_table(outer_t)
    b_hi, b_lo = split_table(inner_t)
    fwd_a = np.concatenate([a_hi, a_lo], 1)
    fwd_b = np.concatenate([b_hi, b_hi, b_lo], 0)
    return fwd_a, twist, fwd_b, b_hi.T, a_hi.T


def split(value):
    high = value.astype(BF16)
    low = (value - high.astype(F32)).astype(BF16)
    return high, low


def mul(left, right):
    return jnp.dot(left, right, preferred_element_type=F32)


def mul_rows(left, right, step):
    parts = [mul(left[i : i + step], right) for i in range(0, left.shape[0], step)]
    return jnp.concatenate(parts, 0)


def to_spectra(cols, fwd_a, twist, fwd_b):
    blocks, width = cols[0].shape
    data = jnp.concatenate(cols, 1)
    part = mul(fwd_a, jnp.concatenate([data, data], 0))
    t_re, t_im = twist[:, :width], twist[:, width:]
    rows = []
    for s in range(len(cols)):
        a_re = part[:blocks, s * width : (s + 1) * width]
        a_im = part[blocks:, s * width : (s + 1) * width]
        rows.append(jnp.concatenate([a_re * t_re - a_im * t_im, a_re * t_im + a_im * t_re], 1))
    high, low = split(jnp.concatenate(rows, 0))
    return mul_rows(jnp.concatenate([high, low, high], 1), fwd_b, 448)


def from_spectra(spec, twist, inv_b, inv_a, scale):
    blocks = twist.shape[0]
    width = twist.shape[1] // 2
    count = spec.shape[0] // blocks
    part = mul_rows(spec.astype(BF16), inv_b, 448)
    t_re, t_im = twist[:, :width], twist[:, width:]
    cols = []
    for s in range(count):
        d_re = part[s * blocks : (s + 1) * blocks, :width]
        d_im = part[s * blocks : (s + 1) * blocks, width:]
        cols.append(jnp.concatenate([d_re * t_re + d_im * t_im, d_im * t_re - d_re * t_im], 0))
    return mul(inv_a, jnp.concatenate(cols, 1).astype(BF16)) * scale


def gate_kernel(repeat, blocks, query, key_in, value, cotangent, taps, out_ref, *scratch):
    hold, sems = scratch[-2], scratch[-1]
    width = taps.shape[0]
    fils = width // blocks
    per = (2 * repeat + 1) * fils
    copies = []
    for i, source in enumerate((key_in, value, taps, cotangent, query)):
        copies.append(pltpu.make_async_copy(source, scratch[i], sems.at[i]))
        copies[-1].start()
    k_in, v_in, t_in, g_in, q_in = scratch[:5]

    def put(first, part):
        flipped = part.T
        for f in range(fils):
            hold[pl.ds(first + f, blocks, stride=per), :] = flipped[f * blocks : (f + 1) * blocks]

    def put_product(first, left, right):
        for c in range(repeat):
            at = slice(c * width, (c + 1) * width)
            prod = left[:, at].astype(F32) * right[:, at].astype(F32)
            put(first + c * fils, prod.astype(BF16).astype(F32))

    copies[0].wait()
    copies[1].wait()
    put_product(0, k_in, v_in)
    copies[2].wait()
    put(2 * repeat * fils, t_in[...].astype(F32))
    copies[3].wait()
    copies[4].wait()
    put_product(repeat * fils, g_in, q_in)
    out_ref[...] = hold[: out_ref.shape[0]].astype(BF16)


def take_columns(ref, hold, per, blocks):
    hold[: ref.shape[0]] = ref[...].astype(F32)
    return [hold[pl.ds(s, blocks, stride=per), :].astype(BF16) for s in range(per)]


def times(a, b):
    w = a.shape[1] // 2
    a_re, a_im, b_re, b_im = a[:, :w], a[:, w:], b[:, :w], b[:, w:]
    return jnp.concatenate([a_re * b_re - a_im * b_im, a_re * b_im + a_im * b_re], 1)


def times_conj(a, b):
    w = a.shape[1] // 2
    a_re, a_im, b_re, b_im = a[:, :w], a[:, w:], b[:, :w], b[:, w:]
    return jnp.concatenate([a_re * b_re + a_im * b_im, a_im * b_re - a_re * b_im], 1)


def core_kernel(repeat, scale, x_ref, fa, tw, fb, ib, ia, out_ref, hold):
    blocks = tw.shape[0]
    width = tw.shape[1] // 2
    per = x_ref.shape[0] // blocks
    fils = per // (2 * repeat + 1)
    step = fils * blocks
    spec = to_spectra(take_columns(x_ref, hold, per, blocks), fa[...], tw[...], fb[...])
    parts = [spec[s * step : (s + 1) * step] for s in range(2 * repeat + 1)]
    mixed, gated, taps = parts[:repeat], parts[repeat : 2 * repeat], parts[-1]
    cross = times_conj(gated[0], mixed[0])
    for s in range(1, repeat):
        cross = cross + times_conj(gated[s], mixed[s])
    prods = [times(m, taps) for m in mixed] + [times_conj(g, taps) for g in gated] + [cross]
    result = from_spectra(jnp.concatenate(prods, 0), tw[...], ib[...], ia[...], scale)
    for s in range(per):
        hold[pl.ds(s, blocks, stride=per), :] = result[:, s * width : (s + 1) * width]
    out_ref[...] = hold[: out_ref.shape[0]].astype(BF16)


def back_rows(rows, first, blocks, width):
    per = rows.shape[0] // blocks
    parts = [rows[pl.ds(first + f, blocks, stride=per), :] for f in range(width // blocks)]
    return jnp.concatenate(parts, 0).T


def taps_kernel(repeat, blocks, group, rows_ref, taps, hold):
    width = taps.shape[1]
    hold[: rows_ref.shape[0]] = rows_ref[...].astype(F32)
    flipped = back_rows(hold, 2 * repeat * (width // blocks), blocks, width).astype(BF16)
    lags = width // len(group)
    for c, owner in enumerate(group):
        taps[c * lags : (c + 1) * lags] = flipped[owner * lags : (owner + 1) * lags]


def grads_kernel(
    repeat, blocks, rows_ref, part_ref, cot, value, key_in, grad_query, grad_key, grad_value, grad_filter, hold
):
    width = cot.shape[0]
    fils = width // blocks
    hold[: rows_ref.shape[0]] = rows_ref[...].astype(F32)
    lags = grad_filter.shape[0]
    total = part_ref[:lags].astype(F32)
    for c in range(1, width // lags):
        total = total + part_ref[c * lags : (c + 1) * lags].astype(F32)
    grad_filter[...] = total
    for c in range(repeat):
        at = slice(c * width, (c + 1) * width)
        conv = back_rows(hold, c * fils, blocks, width)
        grad_query[:, at] = (cot[:, at].astype(F32) * conv).astype(BF16)
        back = back_rows(hold, (repeat + c) * fils, blocks, width)
        grad_key[:, at] = (back * value[:, at].astype(F32)).astype(BF16)
        grad_value[:, at] = (back * key_in[:, at].astype(F32)).astype(BF16)


def local(query, key_in, value, cotangent, filter_raw):
    width, channels = query.shape
    blocks = lax.axis_size("seq")
    groups = lax.axis_size("chan")
    length = blocks * width
    filters = filter_raw.shape[1]
    repeat = channels // filters
    fils = filters // blocks
    per = (2 * repeat + 1) * fils
    scale = 1.0 / (length * math.sqrt(length))
    first = blocks // 2 + 7
    group = [(3 * groups // 4 + c) % groups for c in range(groups)]
    order = [(first - i) % blocks for i in range(blocks)]
    tables = [jnp.asarray(t) for t in make_tables(blocks, width, order)]
    params = pltpu.CompilerParams(vmem_limit_bytes=VMEM_LIMIT)
    packed = jax.ShapeDtypeStruct((blocks * per, width), BF16)
    hold = pltpu.VMEM((blocks * per + 16, width), F32)

    def swap(array):
        shape = (blocks, per // fils, fils, width)
        moved = lax.all_to_all(array.reshape(shape), "seq", split_axis=0, concat_axis=0, tiled=True, axis_index_groups=[order])
        return moved.reshape(array.shape)

    wide = pltpu.VMEM((width, channels), BF16)
    rows = pl.pallas_call(
        functools.partial(gate_kernel, repeat, blocks),
        out_shape=packed,
        in_specs=[pl.BlockSpec(memory_space=pl.ANY)] * 5,
        scratch_shapes=[wide, wide, pltpu.VMEM((width, filters), BF16), wide, wide, hold, pltpu.SemaphoreType.DMA((5,))],
        compiler_params=params,
        name="gate",
    )(*(pltpu.with_memory_space_constraint(a, pltpu.HBM) for a in (query, key_in, value, cotangent, filter_raw)))
    rows = pl.pallas_call(
        functools.partial(core_kernel, repeat, scale),
        out_shape=packed,
        scratch_shapes=[hold],
        compiler_params=params,
        name="core",
    )(swap(rows), *tables)
    rows = swap(rows)
    like = jax.ShapeDtypeStruct((width, channels), BF16)
    taps = pl.pallas_call(
        functools.partial(taps_kernel, repeat, blocks, group),
        out_shape=jax.ShapeDtypeStruct((width, filters), BF16),
        scratch_shapes=[hold],
        compiler_params=params,
        name="taps",
    )(rows)
    taps = lax.all_to_all(taps, "chan", split_axis=0, concat_axis=0, tiled=True, axis_index_groups=[group])
    return pl.pallas_call(
        functools.partial(grads_kernel, repeat, blocks),
        out_shape=(like, like, like, jax.ShapeDtypeStruct((width // groups, filters), F32)),
        scratch_shapes=[hold],
        compiler_params=params,
        name="grads",
    )(rows, taps, cotangent, value, key_in)


def solution(mesh):
    placed = (
        P("seq", "chan"),
        P("seq", "chan"),
        P("seq", "chan"),
        P("seq", "chan"),
        P("seq", None),
    )
    return jax.shard_map(
        local,
        mesh=mesh,
        in_specs=placed,
        out_specs=(P("seq", "chan"), P("seq", "chan"), P("seq", "chan"), P(("seq", "chan"), None)),
        check_vma=False,
    )
```
